32 devices in a mesh: box: 8 (over z, core), samp: 4 (over y, x).
Axes of the slice: x: 2, y: 2, z: 4, core: 2. Of those that a mesh axis runs over, the one named last changes fastest.
Arguments:
- radiation: float32 [2, 256, 88, 168], P(None, 'box', 'samp'), may hold values from -6 to 6
- theta_mid: float32 [160, 88], replicated, may hold values from -0.625 to 0.625
- phi_mid: float32 [312, 168], replicated, may hold values from -0.5 to 0.5
- theta_top: float32 [296, 160], replicated, may hold values from -0.5 to 0.5
- phi_top: float32 [584, 312], replicated, may hold values from -0.3125 to 0.3125
- shift_mid: float32 [8, 160, 312], replicated, may hold values from -3.140625 to 3.140625
- shift_top: float32 [8, 296, 584], replicated, may hold values from -3.140625 to 3.140625
- octant_low: int32 [256], P('box'), may hold values from 0 to 7
- octant_mid: int32 [64], P('box'), may hold values from 0 to 7
- parent_low: int32 [256], P('box'), may hold values from 0 to 63, as said below
- parent_mid: int32 [64], P('box'), may hold values from 0 to 15, as said below
- trans_low: float32 [2, 16, 88, 168], P(None, None, 'samp'), may hold values from -4 to 4
- trans_mid: float32 [2, 16, 160, 312], P(None, None, 'samp'), may hold values from -4 to 4
- trans_top: float32 [2, 16, 296, 584], P(None, None, 'samp'), may hold values from -4 to 4
- far_low: int32 [256, 16], P('box'), may hold values from 0 to 255, as said below
- far_mid: int32 [64, 16], P('box'), may hold values from 0 to 63, as said below
- far_top: int32 [16, 16], P('box'), may hold values from 0 to 15, as said below
- offset_low: int32 [256, 16], P('box'), may hold values from 0 to 15
- offset_mid: int32 [64, 16], P('box'), may hold values from 0 to 15
- offset_top: int32 [16, 16], P('box'), may hold values from 0 to 15
Outputs:
- incoming: float32 [2, 256, 88, 168], P(None, 'box', 'samp')
The draws below stay inside these ranges and needn't reach their ends.
Inputs may be any that keep to these rules, and one draw needn't show every extreme that they name: `parent_low`: each middle box has exactly 4 children; the children of the middle boxes 8 * j to 8 * j + 7 are the finest boxes 32 * j to 32 * j + 31. `parent_mid`: each top box has exactly 4 children; the children of the top boxes 2 * j to 2 * j + 1 are the middle boxes 8 * j to 8 * j + 7. `far_low`: A finest box in the run 32 * j to 32 * j + 31 names only boxes of the runs j - 1, j and j + 1 (those that exist); every box whose run has a lower neighbour run names a box of it, and likewise for a higher one. `far_mid`: A middle box in the run 8 * j to 8 * j + 7 names only boxes of the runs j - 1, j and j + 1 (those that exist); every box whose run has a lower neighbour run names a box of it, and likewise for a higher one. `far_top`: A top box in the run 2 * j to 2 * j + 1 names only boxes of the runs j - 1, j and j + 1 (those that exist); every box whose run has a lower neighbour run names a box of it, and likewise for a higher one.
All inputs are finite; a program needn't handle non-finite values.
Results may differ from the reference program's by a relative error of at most 0.000071.
Values sent between devices are 32-bit elements; how exact they have to be, the bound alone decides.
A program may use at most 192 MiB of HBM per device.

```python
import jax
import jax.numpy as jnp
from jax import lax

BD1 = 32
BD2 = 8
BD3 = 2
TH1 = 88
PH1 = 168
TH2 = 160
PH2 = 312
TH3 = 296
PH3 = 584
FAR = 16
NOFF = 16
NB1 = 256
NB2 = 64
NB3 = 16


def block_parents(key, children, per_block, parents_per_block):
    blocks = children // per_block
    block_keys = jax.random.split(key, blocks)

    def shuffle(single_key):
        return jax.random.permutation(single_key, per_block)
    shuffled = jax.vmap(shuffle)(block_keys)
    within = shuffled % parents_per_block
    first_ids = jnp.arange(blocks, dtype=jnp.int32)[:, None] * parents_per_block
    return (first_ids + within).reshape(children).astype(jnp.int32)


def draw_parent_low(key, part):
    key = jax.random.fold_in(key, 11)
    return block_parents(key, NB1, BD1, BD2)


def draw_parent_mid(key, part):
    key = jax.random.fold_in(key, 23)
    return block_parents(key, NB2, BD2, BD3)


def neighbour_lists(key, count, per_run):
    runs = count // per_run
    keys = jax.random.split(key, 3)
    box_ids = jnp.arange(count, dtype=jnp.int32)
    run_ids = box_ids // per_run
    low_run = jnp.maximum(run_ids - 1, 0)
    high_run = jnp.minimum(run_ids + 2, runs)
    spans = (high_run - low_run) * per_run
    picks = jax.random.randint(keys[0], (count, FAR), 0, spans[:, None], dtype=jnp.int32)
    ids = low_run[:, None] * per_run + picks
    turns = jax.random.randint(keys[1], (runs,), 0, per_run, dtype=jnp.int32)
    turns_up = jax.random.randint(keys[2], (runs,), 0, per_run, dtype=jnp.int32)
    within = box_ids % per_run
    below = (run_ids - 1) * per_run + (within + turns[run_ids]) % per_run
    above = (run_ids + 1) * per_run + (within + turns_up[run_ids]) % per_run
    first_col = jnp.where(run_ids > 0, below, ids[:, 0])
    second_col = jnp.where(run_ids < runs - 1, above, ids[:, 1])
    return jnp.concatenate([first_col[:, None], second_col[:, None], ids[:, 2:]], axis=1).astype(jnp.int32)


def draw_far_low(key, part):
    key = jax.random.fold_in(key, 31)
    return neighbour_lists(key, NB1, BD1)


def draw_far_mid(key, part):
    key = jax.random.fold_in(key, 37)
    return neighbour_lists(key, NB2, BD2)


def draw_far_top(key, part):
    key = jax.random.fold_in(key, 41)
    return neighbour_lists(key, NB3, BD3)


def touch_ends(array, rng, smallest, high):
    longest = array.shape.index(max(array.shape))
    spots = []
    for shift in (0, 1):
        where = [jax.random.randint(jax.random.fold_in(rng, axis), (), 0, length) for axis, length in enumerate(array.shape)]
        where[longest] = (where[longest] + shift) % array.shape[longest]
        spots.append(tuple(where))
    return array.at[spots[0]].set(smallest).at[spots[1]].set(high)


def level_of(own_key, shape, pieces, smallest, largest):
    factor_of, own = 1.0, jax.random.fold_in(own_key, 6)
    for position, parts in pieces:
        heights = jnp.exp(jax.random.uniform(jax.random.fold_in(own, position), (parts,), jnp.float32, smallest / len(pieces), largest / len(pieces)))
        factor_of = factor_of * jnp.repeat(heights, shape[position] // parts).reshape([-1 if axis == position else 1 for axis in range(len(shape))])
    return factor_of


def centred(rng, shape, deviation, reach, shards=(), kind=jnp.bfloat16):
    factor_of = level_of(rng, shape, shards, -0.22, 0.18) if shards else 1.0
    values = jax.random.normal(rng, shape, jnp.float32) * deviation * factor_of
    return jnp.minimum(jnp.maximum(values, -reach), reach).astype(kind)


def setup_inputs(seed: int = 0) -> dict:
    seeds = jax.random.split(jax.random.key(seed), 21)
    return {
        "radiation": centred(seeds[0], (2, NB1, TH1, PH1), 1.0, 6.0, ((1, 8), (2, 4)), jnp.float32),
        "theta_mid": centred(seeds[1], (TH2, TH1), TH1 ** -0.5, 0.625, (), jnp.float32),
        "phi_mid": centred(seeds[2], (PH2, PH1), PH1 ** -0.5, 0.5, (), jnp.float32),
        "theta_top": centred(seeds[3], (TH3, TH2), TH2 ** -0.5, 0.5, (), jnp.float32),
        "phi_top": centred(seeds[4], (PH3, PH2), PH2 ** -0.5, 0.3125, (), jnp.float32),
        "shift_mid": jnp.clip(jax.random.uniform(seeds[5], (8, TH2, PH2), jnp.float32, -3.140625, 3.140625), -3.140625, 3.140625),
        "shift_top": jnp.clip(jax.random.uniform(seeds[6], (8, TH3, PH3), jnp.float32, -3.140625, 3.140625), -3.140625, 3.140625),
        "octant_low": touch_ends(jax.random.randint(seeds[7], (NB1,), 0, 8), jax.random.fold_in(seeds[7], 1), 0, 7).astype(jnp.int32),
        "octant_mid": touch_ends(jax.random.randint(seeds[8], (NB2,), 0, 8), jax.random.fold_in(seeds[8], 1), 0, 7).astype(jnp.int32),
        "parent_low": draw_parent_low(jax.random.fold_in(seeds[20], 71), 0),
        "parent_mid": draw_parent_mid(jax.random.fold_in(seeds[20], 71), 0),
        "trans_low": centred(seeds[11], (2, NOFF, TH1, PH1), 0.3, 4.0, ((2, 4),), jnp.float32),
        "trans_mid": centred(seeds[12], (2, NOFF, TH2, PH2), 0.3, 4.0, ((2, 4),), jnp.float32),
        "trans_top": centred(seeds[13], (2, NOFF, TH3, PH3), 0.3, 4.0, ((2, 4),), jnp.float32),
        "far_low": draw_far_low(jax.random.fold_in(seeds[20], 71), 0),
        "far_mid": draw_far_mid(jax.random.fold_in(seeds[20], 71), 0),
        "far_top": draw_far_top(jax.random.fold_in(seeds[20], 71), 0),
        "offset_low": touch_ends(jax.random.randint(seeds[17], (NB1, FAR), 0, NOFF), jax.random.fold_in(seeds[17], 1), 0, NOFF - 1).astype(jnp.int32),
        "offset_mid": touch_ends(jax.random.randint(seeds[18], (NB2, FAR), 0, NOFF), jax.random.fold_in(seeds[18], 1), 0, NOFF - 1).astype(jnp.int32),
        "offset_top": touch_ends(jax.random.randint(seeds[19], (NB3, FAR), 0, NOFF), jax.random.fold_in(seeds[19], 1), 0, NOFF - 1).astype(jnp.int32),
    }


highest = lax.Precision.HIGHEST


def rotate(real_part, imag_part, cosines, sines):
    return real_part * cosines - imag_part * sines, real_part * sines + imag_part * cosines


def aggregate(patterns, theta_w, phi_w, angles, octant, parent, count):
    interp = jnp.einsum('rbtp,qp->rbtq', patterns, phi_w, precision=highest)
    mixed = jnp.einsum('st,rbtq->rbsq', theta_w, interp, precision=highest)
    cosines = jnp.cos(angles)[octant]
    sines = jnp.sin(angles)[octant]
    real_part, imag_part = rotate(mixed[0], mixed[1], cosines, sines)
    summed_real = jax.ops.segment_sum(real_part, parent, count)
    summed_imag = jax.ops.segment_sum(imag_part, parent, count)
    return jnp.stack([summed_real, summed_imag])


def translate(patterns, table, far_list, offsets):
    def advance(running, columns):
        far_col, off_col = columns
        sources = patterns[:, far_col]
        coeffs = table[:, off_col]
        real_part, imag_part = rotate(sources[0], sources[1], coeffs[0], coeffs[1])
        return running + jnp.stack([real_part, imag_part]), None

    initial = jnp.zeros(patterns.shape, jnp.float32)
    result, _ = lax.scan(advance, initial, (far_list.T, offsets.T))
    return result


def disaggregate(patterns, theta_w, phi_w, angles, octant, parent):
    spread = patterns[:, parent]
    cosines = jnp.cos(angles)[octant]
    sines = jnp.sin(angles)[octant]
    real_part, imag_part = rotate(spread[0], spread[1], cosines, -sines)
    shifted = jnp.stack([real_part, imag_part])
    mixed = jnp.einsum('st,rcsq->rctq', theta_w, shifted, precision=highest)
    return jnp.einsum('rctq,qp->rctp', mixed, phi_w, precision=highest)


def reference(radiation, theta_mid, phi_mid, theta_top, phi_top, shift_mid, shift_top, octant_low, octant_mid, parent_low, parent_mid, trans_low, trans_mid, trans_top, far_low, far_mid, far_top, offset_low, offset_mid, offset_top):
    middle = aggregate(radiation, theta_mid, phi_mid, shift_mid, octant_low, parent_low, NB2)
    summit = aggregate(middle, theta_top, phi_top, shift_top, octant_mid, parent_mid, NB3)
    in_top = translate(summit, trans_top, far_top, offset_top)
    in_mid = translate(middle, trans_mid, far_mid, offset_mid) + disaggregate(in_top, theta_top, phi_top, shift_top, octant_mid, parent_mid)
    return translate(radiation, trans_low, far_low, offset_low) + disaggregate(in_mid, theta_mid, phi_mid, shift_mid, octant_low, parent_low)
```

```python
import functools

import jax
import jax.numpy as jnp
from jax import lax
from jax.experimental import pallas as pl
from jax.experimental.pallas import tpu as pltpu
from jax.sharding import PartitionSpec as P

VMEM_LIMIT = 48 * 1024 * 1024
VMEM = pltpu.VMEM
SMEM = pltpu.SMEM


def sincos(angle):
    half = 0.5 * angle
    z = half * half
    s = jnp.float32(1.0 / 6227020800.0)
    for c in (-1.0 / 39916800.0, 1.0 / 362880.0, -1.0 / 5040.0, 1.0 / 120.0, -1.0 / 6.0, 1.0):
        s = s * z + c
    s = s * half
    k = jnp.float32(1.0 / 479001600.0)
    for c in (-1.0 / 3628800.0, 1.0 / 40320.0, -1.0 / 720.0, 1.0 / 24.0, -0.5, 1.0):
        k = k * z + c
    return 2.0 * s * k, 1.0 - 2.0 * s * s


def split(x):
    high = x.astype(jnp.bfloat16)
    return high, (x - high.astype(jnp.float32)).astype(jnp.bfloat16)


def dot3(a, b):
    (ah, al), (bh, bl) = split(a), split(b)
    dot = functools.partial(jnp.dot, preferred_element_type=jnp.float32)
    return dot(ah, bl) + dot(al, bh) + dot(ah, bh)


def up_kernel(n, kids, oct_ref, x_ref, q_ref, rt_ref, shift_ref, out_ref, x_all, mixed):
    i = pl.program_id(0)
    rows = x_ref.shape[3]
    theta = n * rows
    rows_out = out_ref.shape[3]
    for r in range(2):
        for k in range(n):
            x_all[r * theta + k * rows:r * theta + (k + 1) * rows, :] = x_ref[k, r, 0]
    interp = dot3(x_all[...], rt_ref[...])
    q = q_ref[...]
    real = dot3(q, interp[:theta])
    imag = dot3(q, interp[theta:])
    sine, cosine = sincos(shift_ref[0])
    turned = (real * cosine - imag * sine, real * sine + imag * cosine)
    child = lax.rem(i, kids)

    @pl.when(child == 0)
    def _():
        for r in range(2):
            mixed[r] = turned[r]

    @pl.when(child > 0)
    def _():
        for r in range(2):
            mixed[r] = mixed[r] + turned[r]

    @pl.when(child == kids - 1)
    def _():
        for r in range(2):
            for k in range(n):
                out_ref[k, r, 0] = mixed[r, k * rows_out:(k + 1) * rows_out, :]


def go_up(x, theta_w, phi_w, angles, octant, parents):
    n, _, boxes, rows, p = x.shape
    s, q = theta_w.shape[0], phi_w.shape[0]
    kids = boxes // parents
    spec = pltpu.PrefetchScalarGridSpec(
        num_scalar_prefetch=1,
        grid=(boxes,),
        in_specs=[
            pl.BlockSpec((n, 2, 1, rows, p), lambda i, o: (0, 0, i, 0, 0)),
            pl.BlockSpec((s, n * rows), lambda i, o: (0, 0)),
            pl.BlockSpec((p, q), lambda i, o: (0, 0)),
            pl.BlockSpec((1, s, q), lambda i, o: (o[i], 0, 0)),
        ],
        out_specs=pl.BlockSpec((n, 2, 1, s // n, q), lambda i, o: (0, 0, i // kids, 0, 0)),
        scratch_shapes=[
            pltpu.VMEM((2 * n * rows, p), jnp.float32),
            pltpu.VMEM((2, s, q), jnp.float32),
        ],
    )
    return pl.pallas_call(
        functools.partial(up_kernel, n, kids),
        grid_spec=spec,
        out_shape=jax.ShapeDtypeStruct((n, 2, parents, s // n, q), jnp.float32),
        compiler_params=pltpu.CompilerParams(vmem_limit_bytes=VMEM_LIMIT),
    )(octant, x, theta_w, phi_w.T, angles)


def down_kernel(n, kids, with_add, oct_ref, g_ref, qt_ref, r_ref, shift_ref, *rest):
    if with_add:
        add_ref, out_ref, held, mixed, final = rest
    else:
        out_ref, held, mixed, final = rest
    i = pl.program_id(0)
    rows = g_ref.shape[3]
    theta = qt_ref.shape[0]
    rows_out = theta // n

    @pl.when(lax.rem(i, kids) == 0)
    def _():
        for r in range(2):
            for k in range(n):
                held[r, k * rows:(k + 1) * rows, :] = g_ref[k, r, 0]

    sine, cosine = sincos(shift_ref[0])
    real, imag = held[0], held[1]
    qt = qt_ref[...]
    mixed[:theta, :] = dot3(qt, real * cosine + imag * sine)
    mixed[theta:, :] = dot3(qt, imag * cosine - real * sine)
    final[...] = dot3(mixed[...], r_ref[...])
    for r in range(2):
        for k in range(n):
            part = final[r * theta + k * rows_out:r * theta + (k + 1) * rows_out, :]
            out_ref[k, r, 0] = part + add_ref[k, r, 0] if with_add else part


def go_down(g, theta_w, phi_w, angles, octant, add):
    n, _, parents, rows, q = g.shape
    boxes = octant.shape[0]
    kids = boxes // parents
    s, t = theta_w.shape
    p = phi_w.shape[1]
    block_out = pl.BlockSpec((n, 2, 1, t // n, p), lambda i, o: (0, 0, i, 0, 0))
    with_add = add is not None
    spec = pltpu.PrefetchScalarGridSpec(
        num_scalar_prefetch=1,
        grid=(boxes,),
        in_specs=[
            pl.BlockSpec((n, 2, 1, rows, q), lambda i, o: (0, 0, i // kids, 0, 0)),
            pl.BlockSpec((t, s), lambda i, o: (0, 0)),
            pl.BlockSpec((q, p), lambda i, o: (0, 0)),
            pl.BlockSpec((1, s, q), lambda i, o: (o[i], 0, 0)),
        ] + ([block_out] if with_add else []),
        out_specs=block_out,
        scratch_shapes=[
            pltpu.VMEM((2, s, q), jnp.float32),
            pltpu.VMEM((2 * t, q), jnp.float32),
            pltpu.VMEM((2 * t, p), jnp.float32),
        ],
    )
    args = (octant, g, theta_w.T, phi_w, angles) + ((add,) if with_add else ())
    return pl.pallas_call(
        functools.partial(down_kernel, n, kids, with_add),
        grid_spec=spec,
        out_shape=jax.ShapeDtypeStruct((n, 2, boxes, t // n, p), jnp.float32),
        compiler_params=pltpu.CompilerParams(vmem_limit_bytes=VMEM_LIMIT),
    )(*args)


def translate_kernel(boxes, group, noff, with_add, chunk, e_ref, o_ref, *rest):
    if with_add:
        a_ref, pat, tab, add_ref, out_ref = rest
    else:
        pat, tab, out_ref = rest
    rows = pat.shape[1]
    far = e_ref.shape[1]

    def step(b, carry):
        place = (b // group) * (2 * group) + lax.rem(b, group)
        for lo in range(0, rows, chunk):
            here = slice(lo, min(lo + chunk, rows))
            if with_add:
                start = a_ref[b]
                real = add_ref[start, here, :]
                imag = add_ref[start + with_add, here, :]
            else:
                real = imag = None
            for f in range(far):
                e, o = e_ref[b, f], o_ref[b, f]
                sr, si = pat[e, here, :], pat[e + boxes, here, :]
                cr, ci = tab[o, here, :], tab[o + noff, here, :]
                dr, di = sr * cr - si * ci, sr * ci + si * cr
                real = dr if real is None else real + dr
                imag = di if imag is None else imag + di
            out_ref[place, here, :] = real
            out_ref[place + group, here, :] = imag
        return carry

    lax.fori_loop(0, boxes, step, 0)


def translate(near, table, far_ids, offsets, group, add=None, add_at=None, add_group=0):
    _, _, boxes, rows, p = near.shape
    noff = table.shape[1]
    chunk = 24 if p <= 256 else 16 if p <= 384 else 8
    first = (lax.axis_index("box") - 1) * boxes
    local = far_ids - first
    entry = (local // boxes) * (2 * boxes) + local % boxes
    args = [entry, offsets]
    specs = [pl.BlockSpec(memory_space=SMEM)] * 2
    if add is not None:
        args.append((add_at // add_group) * (2 * add_group) + add_at % add_group)
        specs.append(pl.BlockSpec(memory_space=SMEM))
    args += [near.reshape(6 * boxes, rows, p), table.reshape(2 * noff, rows, p)]
    specs += [pl.BlockSpec(memory_space=VMEM)] * 2
    if add is not None:
        args.append(add.reshape(-1, rows, p))
        specs.append(pl.BlockSpec(memory_space=VMEM))
    out = pl.pallas_call(
        functools.partial(translate_kernel, boxes, group, noff, add_group, chunk),
        in_specs=specs,
        out_specs=pl.BlockSpec(memory_space=VMEM),
        out_shape=jax.ShapeDtypeStruct((2 * boxes, rows, p), jnp.float32),
        compiler_params=pltpu.CompilerParams(vmem_limit_bytes=VMEM_LIMIT),
    )(*args)
    return out.reshape(boxes // group, 2, group, rows, p)


def exchange_kernel(n, runs, swaps, halos, shares, *refs):
    count = swaps + halos
    xs, ys = refs[:count], refs[count:2 * count]
    send, recv, own, halo_send, halo_recv = refs[2 * count:]
    me = lax.axis_index("samp")
    box = lax.axis_index("box")
    barrier = pltpu.get_barrier_semaphore()
    has_low, has_high = box > 0, box < runs - 1
    low, high = jnp.maximum(box - 1, 0), jnp.minimum(box + 1, runs - 1)
    mesh = pl.DeviceIdType.MESH
    if swaps:
        for d in range(1, n):
            peer = lax.rem(me + d, n)
            pl.semaphore_signal(barrier, 1, device_id={"samp": peer}, device_id_type=mesh)
    if halos:
        @pl.when(has_low)
        def _():
            pl.semaphore_signal(barrier, 1, device_id={"box": low}, device_id_type=mesh)

        @pl.when(has_high)
        def _():
            pl.semaphore_signal(barrier, 1, device_id={"box": high}, device_id_type=mesh)
    arrivals = n - 1 if swaps else 0
    if halos:
        arrivals = arrivals + has_low.astype(jnp.int32) + has_high.astype(jnp.int32)
    pl.semaphore_wait(barrier, arrivals)
    copies, locals_, ups, downs = [], [], [], []
    for j in range(halos):
        x, y = xs[swaps + j], ys[swaps + j]
        up = pltpu.make_async_remote_copy(
            x, y.at[0], halo_send.at[j, 0], halo_recv.at[j, 0],
            device_id={"box": high}, device_id_type=mesh)
        down = pltpu.make_async_remote_copy(
            x, y.at[2], halo_send.at[j, 1], halo_recv.at[j, 1],
            device_id={"box": low}, device_id_type=mesh)
        pl.when(has_high)(up.start)
        pl.when(has_low)(down.start)
        ups.append(up)
        downs.append(down)
    for d in [2, 1, 3] if n == 4 else range(1, n):
        for j in range(swaps):
            peer = lax.rem(me + d, n)
            copy = pltpu.make_async_remote_copy(
                xs[j].at[peer // shares[j]], ys[j].at[me], send.at[j, d], recv.at[j, d],
                device_id={"samp": peer}, device_id_type=mesh)
            copy.start()
            copies.append(copy)
    for j in range(count):
        if j < swaps:
            copy = pltpu.make_async_copy(xs[j].at[me // shares[j]], ys[j].at[me], own.at[j])
        else:
            copy = pltpu.make_async_copy(xs[j], ys[j].at[1], own.at[j])
        copy.start()
        locals_.append(copy)
    for copy in locals_ + copies:
        copy.wait()
    for up, down in zip(ups, downs):
        pl.when(has_high)(up.wait_send)
        pl.when(has_low)(down.wait_send)
        pl.when(has_low)(up.wait_recv)
        pl.when(has_high)(down.wait_recv)


def exchange(number, swaps, halos):
    n, runs = lax.axis_size("samp"), lax.axis_size("box")
    arrays = [x for x, _ in swaps] + list(halos)
    shapes = [jax.ShapeDtypeStruct((n,) + x.shape[1:], x.dtype) for x, _ in swaps]
    shapes += [jax.ShapeDtypeStruct((3,) + x.shape, x.dtype) for x in halos]
    dma = pltpu.SemaphoreType.DMA
    return pl.pallas_call(
        functools.partial(
            exchange_kernel, n, runs, len(swaps), len(halos), tuple(s for _, s in swaps)),
        in_specs=[pl.BlockSpec(memory_space=pl.ANY)] * len(arrays),
        out_specs=[pl.BlockSpec(memory_space=pl.ANY)] * len(arrays),
        out_shape=shapes,
        scratch_shapes=[
            dma((max(len(swaps), 1), n)),
            dma((max(len(swaps), 1), n)),
            dma((len(arrays),)),
            dma((max(len(halos), 1), 2)),
            dma((max(len(halos), 1), 2)),
        ],
        compiler_params=pltpu.CompilerParams(
            collective_id=number, has_side_effects=True, vmem_limit_bytes=VMEM_LIMIT),
    )(*arrays)


def ranks(key):
    count = key.shape[0]
    ids = jnp.arange(count, dtype=jnp.int32)
    before = (key[None, :] < key[:, None]) | (
        (key[None, :] == key[:, None]) & (ids[None, :] < ids[:, None]))
    rank = jnp.sum(before.astype(jnp.int32), axis=1)
    order = jnp.sum(jnp.where(rank[None, :] == ids[:, None], ids[None, :], 0), axis=1)
    return rank, order


def pick(values, index):
    hot = index[:, None] == jnp.arange(values.shape[0], dtype=jnp.int32)[None, :]
    return jnp.sum(jnp.where(hot, values[None, :], 0), axis=1)


def body(
    radiation, theta_mid, phi_mid, theta_top, phi_top, shift_mid, shift_top,
    octant_low, octant_mid, parent_low, parent_mid, trans_low, trans_mid, trans_top,
    far_low, far_mid, far_top, offset_low, offset_mid, offset_top,
):
    n = lax.axis_size("samp")
    me, box = lax.axis_index("samp"), lax.axis_index("box")
    lows, mids = octant_low.shape[0], octant_mid.shape[0]
    tops = mids // 4
    low_each, mid_each, share = lows // n, mids // n, n // tops
    _, _, rows_low, p_low = radiation.shape
    rank_mid, order_mid = ranks(parent_mid)
    rank_low, order_low = ranks(pick(rank_mid, parent_low - box * mids))
    oct_low = lax.dynamic_slice_in_dim(pick(octant_low, order_low), me * low_each, low_each)
    oct_mid = lax.dynamic_slice_in_dim(pick(octant_mid, order_mid), me * mid_each, mid_each)

    grouped = jnp.take(radiation, order_low, axis=1)
    grouped = jnp.moveaxis(grouped.reshape(2, n, low_each, rows_low, p_low), 1, 0)
    low_parts, near_low = exchange(0, [(grouped, 1)], [radiation])
    mid_parts = go_up(low_parts, theta_mid, phi_mid, shift_mid, oct_low, mid_each)
    mid_rows, = exchange(1, [(mid_parts, 1)], [])
    top_parts = go_up(mid_parts, theta_top, phi_top, shift_top, oct_mid, 1)
    middle = jnp.moveaxis(mid_rows, 0, 1).reshape(2, mids, *mid_rows.shape[3:])
    middle = jnp.take(middle, rank_mid, axis=1)
    top_rows, near_mid = exchange(2, [(top_parts, 1)], [middle])
    summit = top_rows.reshape(tops, share, 2, *top_rows.shape[3:]).sum(axis=1)
    summit = jnp.moveaxis(summit, 0, 1)
    near_top, = exchange(3, [], [summit])
    in_mid = translate(near_mid, trans_mid, far_mid[order_mid], offset_mid[order_mid], mid_each)
    in_top = translate(near_top, trans_top, far_top, offset_top, 1)
    top_here, mid_here = exchange(4, [(in_top, share), (in_mid, 1)], [])
    mid_in = go_down(top_here, theta_top, phi_top, shift_top, oct_mid, mid_here)
    low_in = go_down(mid_in, theta_mid, phi_mid, shift_mid, oct_low, None)
    low_rows, = exchange(5, [(low_in, 1)], [])
    out = translate(
        near_low, trans_low, far_low, offset_low, lows, low_rows, rank_low, low_each)
    return out.reshape(2, lows, rows_low, p_low)


def solution(mesh):
    in_specs = (
        P(None, "box", "samp", None),
        P(), P(), P(), P(), P(), P(),
        P("box"), P("box"), P("box"), P("box"),
        P(None, None, "samp", None),
        P(None, None, "samp", None),
        P(None, None, "samp", None),
        P("box", None), P("box", None), P("box", None),
        P("box", None), P("box", None), P("box", None),
    )
    out_specs = P(None, "box", "samp", None)
    return jax.shard_map(body, mesh=mesh, in_specs=in_specs, out_specs=out_specs, check_vma=False)
```

```python
import functools

import jax
import jax.numpy as jnp
from jax import lax
from jax.experimental import pallas as pl
from jax.experimental.pallas import tpu as pltpu
from jax.sharding import PartitionSpec as P

VMEM_LIMIT = 48 * 1024 * 1024
VMEM = pltpu.VMEM
SMEM = pltpu.SMEM


def sincos(angle):
    half = 0.5 * angle
    z = half * half
    s = jnp.float32(1.0 / 6227020800.0)
    for c in (-1.0 / 39916800.0, 1.0 / 362880.0, -1.0 / 5040.0, 1.0 / 120.0, -1.0 / 6.0, 1.0):
        s = s * z + c
    s = s * half
    k = jnp.float32(1.0 / 479001600.0)
    for c in (-1.0 / 3628800.0, 1.0 / 40320.0, -1.0 / 720.0, 1.0 / 24.0, -0.5, 1.0):
        k = k * z + c
    return 2.0 * s * k, 1.0 - 2.0 * s * s


def split(x):
    high = x.astype(jnp.bfloat16)
    return high, (x - high.astype(jnp.float32)).astype(jnp.bfloat16)


def dot3(a, b):
    (ah, al), (bh, bl) = split(a), split(b)
    dot = functools.partial(jnp.dot, preferred_element_type=jnp.float32)
    return dot(ah, bl) + dot(al, bh) + dot(ah, bh)


def up_kernel(n, kids, oct_ref, x_ref, q_ref, rt_ref, shift_ref, out_ref, x_all, mixed):
    i = pl.program_id(0)
    rows = x_ref.shape[3]
    theta = n * rows
    rows_out = out_ref.shape[3]
    for r in range(2):
        for k in range(n):
            x_all[r * theta + k * rows:r * theta + (k + 1) * rows, :] = x_ref[k, r, 0]
    interp = dot3(x_all[...], rt_ref[...])
    q = q_ref[...]
    real = dot3(q, interp[:theta])
    imag = dot3(q, interp[theta:])
    sine, cosine = sincos(shift_ref[0])
    turned = (real * cosine - imag * sine, real * sine + imag * cosine)
    child = lax.rem(i, kids)

    @pl.when(child == 0)
    def _():
        for r in range(2):
            mixed[r] = turned[r]

    @pl.when(child > 0)
    def _():
        for r in range(2):
            mixed[r] = mixed[r] + turned[r]

    @pl.when(child == kids - 1)
    def _():
        for r in range(2):
            for k in range(n):
                out_ref[k, r, 0] = mixed[r, k * rows_out:(k + 1) * rows_out, :]


def go_up(x, theta_w, phi_w, angles, octant, parents):
    n, _, boxes, rows, p = x.shape
    s, q = theta_w.shape[0], phi_w.shape[0]
    kids = boxes // parents
    spec = pltpu.PrefetchScalarGridSpec(
        num_scalar_prefetch=1,
        grid=(boxes,),
        in_specs=[
            pl.BlockSpec((n, 2, 1, rows, p), lambda i, o: (0, 0, i, 0, 0)),
            pl.BlockSpec((s, n * rows), lambda i, o: (0, 0)),
            pl.BlockSpec((p, q), lambda i, o: (0, 0)),
            pl.BlockSpec((1, s, q), lambda i, o: (o[i], 0, 0)),
        ],
        out_specs=pl.BlockSpec((n, 2, 1, s // n, q), lambda i, o: (0, 0, i // kids, 0, 0)),
        scratch_shapes=[
            pltpu.VMEM((2 * n * rows, p), jnp.float32),
            pltpu.VMEM((2, s, q), jnp.float32),
        ],
    )
    return pl.pallas_call(
        functools.partial(up_kernel, n, kids),
        grid_spec=spec,
        out_shape=jax.ShapeDtypeStruct((n, 2, parents, s // n, q), jnp.float32),
        compiler_params=pltpu.CompilerParams(vmem_limit_bytes=VMEM_LIMIT),
    )(octant, x, theta_w, phi_w.T, angles)


def down_kernel(n, kids, with_add, oct_ref, g_ref, qt_ref, r_ref, shift_ref, *rest):
    if with_add:
        add_ref, out_ref, held, mixed, final = rest
    else:
        out_ref, held, mixed, final = rest
    i = pl.program_id(0)
    rows = g_ref.shape[3]
    theta = qt_ref.shape[0]
    rows_out = theta // n

    @pl.when(lax.rem(i, kids) == 0)
    def _():
        for r in range(2):
            for k in range(n):
                held[r, k * rows:(k + 1) * rows, :] = g_ref[k, r, 0]

    sine, cosine = sincos(shift_ref[0])
    real, imag = held[0], held[1]
    qt = qt_ref[...]
    mixed[:theta, :] = dot3(qt, real * cosine + imag * sine)
    mixed[theta:, :] = dot3(qt, imag * cosine - real * sine)
    final[...] = dot3(mixed[...], r_ref[...])
    for r in range(2):
        for k in range(n):
            part = final[r * theta + k * rows_out:r * theta + (k + 1) * rows_out, :]
            out_ref[k, r, 0] = part + add_ref[k, r, 0] if with_add else part


def go_down(g, theta_w, phi_w, angles, octant, add):
    n, _, parents, rows, q = g.shape
    boxes = octant.shape[0]
    kids = boxes // parents
    s, t = theta_w.shape
    p = phi_w.shape[1]
    block_out = pl.BlockSpec((n, 2, 1, t // n, p), lambda i, o: (0, 0, i, 0, 0))
    with_add = add is not None
    spec = pltpu.PrefetchScalarGridSpec(
        num_scalar_prefetch=1,
        grid=(boxes,),
        in_specs=[
            pl.BlockSpec((n, 2, 1, rows, q), lambda i, o: (0, 0, i // kids, 0, 0)),
            pl.BlockSpec((t, s), lambda i, o: (0, 0)),
            pl.BlockSpec((q, p), lambda i, o: (0, 0)),
            pl.BlockSpec((1, s, q), lambda i, o: (o[i], 0, 0)),
        ] + ([block_out] if with_add else []),
        out_specs=block_out,
        scratch_shapes=[
            pltpu.VMEM((2, s, q), jnp.float32),
            pltpu.VMEM((2 * t, q), jnp.float32),
            pltpu.VMEM((2 * t, p), jnp.float32),
        ],
    )
    args = (octant, g, theta_w.T, phi_w, angles) + ((add,) if with_add else ())
    return pl.pallas_call(
        functools.partial(down_kernel, n, kids, with_add),
        grid_spec=spec,
        out_shape=jax.ShapeDtypeStruct((n, 2, boxes, t // n, p), jnp.float32),
        compiler_params=pltpu.CompilerParams(vmem_limit_bytes=VMEM_LIMIT),
    )(*args)


def sum_far(boxes, noff, chunk, b, e_ref, o_ref, pat, tab, store):
    rows = pat.shape[1]
    for lo in range(0, rows, chunk):
        here = slice(lo, min(lo + chunk, rows))
        real = imag = None
        for f in range(e_ref.shape[1]):
            e, o = e_ref[b, f], o_ref[b, f]
            sr, si = pat[e, here, :], pat[e + boxes, here, :]
            cr, ci = tab[o, here, :], tab[o + noff, here, :]
            dr, di = sr * cr - si * ci, sr * ci + si * cr
            real = dr if real is None else real + dr
            imag = di if imag is None else imag + di
        store(here, real, imag)


def chunk_of(p):
    return 24 if p <= 256 else 16 if p <= 384 else 8


def entries(far_ids, boxes):
    local = far_ids - (lax.axis_index("box") - 1) * boxes
    return (local // boxes) * (2 * boxes) + local % boxes


MESH = pl.DeviceIdType.MESH


def peers_of(n):
    me = lax.axis_index("samp")
    return [(d, lax.rem(me + d, n)) for d in ([2, 1, 3] if n == 4 else range(1, n))]


def greet(n, runs, halos):
    barrier = pltpu.get_barrier_semaphore()
    for _, peer in peers_of(n):
        pl.semaphore_signal(barrier, 1, device_id={"samp": peer}, device_id_type=MESH)
    arrivals = n - 1
    if halos:
        box = lax.axis_index("box")
        has_low, has_high = box > 0, box < runs - 1

        @pl.when(has_low)
        def _():
            pl.semaphore_signal(barrier, 1, device_id={"box": box - 1}, device_id_type=MESH)

        @pl.when(has_high)
        def _():
            pl.semaphore_signal(barrier, 1, device_id={"box": box + 1}, device_id_type=MESH)

        arrivals = arrivals + has_low.astype(jnp.int32) + has_high.astype(jnp.int32)
    pl.semaphore_wait(barrier, arrivals)


def halo_copies(runs, near, size, send, recv):
    box = lax.axis_index("box")
    has_low, has_high = box > 0, box < runs - 1
    own = near.at[pl.ds(size, size)]
    up = pltpu.make_async_remote_copy(
        own, near.at[pl.ds(0, size)], send.at[0], recv.at[0],
        device_id={"box": jnp.minimum(box + 1, runs - 1)}, device_id_type=MESH)
    down = pltpu.make_async_remote_copy(
        own, near.at[pl.ds(2 * size, size)], send.at[1], recv.at[1],
        device_id={"box": jnp.maximum(box - 1, 0)}, device_id_type=MESH)

    def start():
        pl.when(has_high)(up.start)
        pl.when(has_low)(down.start)

    def arrive():
        pl.when(has_low)(up.wait_recv)
        pl.when(has_high)(down.wait_recv)

    def leave():
        pl.when(has_high)(up.wait_send)
        pl.when(has_low)(down.wait_send)

    return start, arrive, leave


def middle_kernel(
    n, runs, e_mid, o_mid, rank, e_top, o_top, top_parts, mid_rows, tab_mid, tab_top,
    top_here, mid_here, near_mid, near_top, top_rows, in_mid, in_top,
    send, recv, halo_send, halo_recv,
):
    me = lax.axis_index("samp")
    mids, tops = e_mid.shape[0], e_top.shape[0]
    each, share = mids // n, n // tops
    noff = tab_mid.shape[0] // 2
    greet(n, runs, True)

    def swap(j, src, dst, share):
        copies = [
            pltpu.make_async_remote_copy(
                src.at[peer // share], dst.at[me], send.at[j, d], recv.at[j, d],
                device_id={"samp": peer}, device_id_type=MESH)
            for d, peer in peers_of(n)
        ]
        for copy in copies:
            copy.start()
        return copies

    tops_out = swap(0, top_parts, top_rows, 1)

    def natural(b, carry):
        place = rank[b]
        for r in range(2):
            near_mid[(2 + r) * mids + b] = mid_rows[place // each, r, lax.rem(place, each)]
        return carry

    lax.fori_loop(0, mids, natural, 0)
    start_mid, mid_arrives, mid_leaves = halo_copies(
        runs, near_mid, 2 * mids, halo_send.at[0], halo_recv.at[0])
    start_mid()
    top_rows[me] = top_parts[me]
    mid_arrives()

    def far_mid(b, carry):
        def store(here, real, imag):
            in_mid[b // each, 0, lax.rem(b, each), here, :] = real
            in_mid[b // each, 1, lax.rem(b, each), here, :] = imag

        sum_far(mids, noff, chunk_of(tab_mid.shape[2]), b, e_mid, o_mid, near_mid, tab_mid, store)
        return carry

    lax.fori_loop(0, mids, far_mid, 0)
    for copy in tops_out:
        copy.wait()
    mids_out = swap(1, in_mid, mid_here, 1)
    mid_here[me] = in_mid[me]
    for t in range(tops):
        for r in range(2):
            total = top_rows[t * share, r, 0]
            for k in range(1, share):
                total = total + top_rows[t * share + k, r, 0]
            near_top[(2 + r) * tops + t] = total
    start_top, top_arrives, top_leaves = halo_copies(
        runs, near_top, 2 * tops, halo_send.at[1], halo_recv.at[1])
    start_top()
    top_arrives()

    def far_top(b, carry):
        def store(here, real, imag):
            in_top[b, 0, 0, here, :] = real
            in_top[b, 1, 0, here, :] = imag

        sum_far(tops, noff, chunk_of(tab_top.shape[2]), b, e_top, o_top, near_top, tab_top, store)
        return carry

    lax.fori_loop(0, tops, far_top, 0)
    tops_back = swap(2, in_top, top_here, share)
    top_here[me] = in_top[me // share]
    for copy in mids_out + tops_back:
        copy.wait()
    mid_leaves()
    top_leaves()


def flat(x, lead):
    return x.reshape((-1,) + x.shape[lead:])


def middle_stage(number, mid_rows, top_parts, rank, trans_mid, trans_top, e_mid, o_mid, e_top, o_top):
    n, runs = lax.axis_size("samp"), lax.axis_size("box")
    mids, tops = e_mid.shape[0], e_top.shape[0]
    f32, dma = jnp.float32, pltpu.SemaphoreType.DMA
    row_mid, row_top = mid_rows.shape[3:], top_parts.shape[3:]
    spec = pl.BlockSpec(memory_space=VMEM)
    return pl.pallas_call(
        functools.partial(middle_kernel, n, runs),
        in_specs=[pl.BlockSpec(memory_space=SMEM)] * 5 + [spec] * 4,
        out_specs=[spec, spec],
        out_shape=[
            jax.ShapeDtypeStruct(top_parts.shape, f32),
            jax.ShapeDtypeStruct(mid_rows.shape, f32),
        ],
        scratch_shapes=[
            pltpu.VMEM((6 * mids,) + row_mid, f32),
            pltpu.VMEM((6 * tops,) + row_top, f32),
            pltpu.VMEM(top_parts.shape, f32),
            pltpu.VMEM(mid_rows.shape, f32),
            pltpu.VMEM((tops, 2, 1) + row_top, f32),
            dma((3, n)), dma((3, n)), dma((2, 2)), dma((2, 2)),
        ],
        compiler_params=pltpu.CompilerParams(
            collective_id=number, has_side_effects=True, vmem_limit_bytes=VMEM_LIMIT),
    )(e_mid, o_mid, rank, e_top, o_top, top_parts, mid_rows, flat(trans_mid, 2), flat(trans_top, 2))


def last_kernel(n, runs, e_ref, o_ref, at_ref, low_in, pat, tab, out_ref, landed, send, recv):
    me = lax.axis_index("samp")
    boxes = e_ref.shape[0]
    size = low_in.shape[0] // n
    noff = tab.shape[0] // 2
    greet(n, runs, False)
    copies = [
        pltpu.make_async_remote_copy(
            low_in.at[pl.ds(peer * size, size)], landed.at[pl.ds(me * size, size)],
            send.at[d], recv.at[d], device_id={"samp": peer}, device_id_type=MESH)
        for d, peer in peers_of(n)
    ]
    for copy in copies:
        copy.start()
    landed[pl.ds(me * size, size)] = low_in[pl.ds(me * size, size)]

    def far(b, carry):
        def store(here, real, imag):
            out_ref[b, here, :] = real
            out_ref[b + boxes, here, :] = imag

        sum_far(boxes, noff, chunk_of(tab.shape[2]), b, e_ref, o_ref, pat, tab, store)
        return carry

    lax.fori_loop(0, boxes, far, 0)
    for copy in copies:
        copy.wait()

    def add(b, carry):
        place = at_ref[b]
        out_ref[b] = out_ref[b] + landed[place]
        out_ref[b + boxes] = out_ref[b + boxes] + landed[place + size // 2]
        return carry

    lax.fori_loop(0, boxes, add, 0)


def last_stage(number, low_in, near, table, e_low, o_low, rank):
    n, runs = lax.axis_size("samp"), lax.axis_size("box")
    boxes, each = e_low.shape[0], low_in.shape[2]
    row = low_in.shape[3:]
    place = (rank // each) * (2 * each) + rank % each
    dma = pltpu.SemaphoreType.DMA
    spec = pl.BlockSpec(memory_space=VMEM)
    return pl.pallas_call(
        functools.partial(last_kernel, n, runs),
        in_specs=[pl.BlockSpec(memory_space=SMEM)] * 3 + [spec] * 3,
        out_specs=spec,
        out_shape=jax.ShapeDtypeStruct((2 * boxes,) + row, jnp.float32),
        scratch_shapes=[pltpu.VMEM((2 * boxes,) + row, jnp.float32), dma((n,)), dma((n,))],
        compiler_params=pltpu.CompilerParams(
            collective_id=number, has_side_effects=True, vmem_limit_bytes=VMEM_LIMIT),
    )(e_low, o_low, place, flat(low_in, 3), flat(near, 3), flat(table, 2)).reshape((2, boxes) + row)


def exchange_kernel(n, runs, swaps, halos, shares, *refs):
    count = swaps + halos
    xs, ys = refs[:count], refs[count:2 * count]
    send, recv, own, halo_send, halo_recv = refs[2 * count:]
    me = lax.axis_index("samp")
    box = lax.axis_index("box")
    barrier = pltpu.get_barrier_semaphore()
    has_low, has_high = box > 0, box < runs - 1
    low, high = jnp.maximum(box - 1, 0), jnp.minimum(box + 1, runs - 1)
    mesh = pl.DeviceIdType.MESH
    if swaps:
        for d in range(1, n):
            peer = lax.rem(me + d, n)
            pl.semaphore_signal(barrier, 1, device_id={"samp": peer}, device_id_type=mesh)
    if halos:
        @pl.when(has_low)
        def _():
            pl.semaphore_signal(barrier, 1, device_id={"box": low}, device_id_type=mesh)

        @pl.when(has_high)
        def _():
            pl.semaphore_signal(barrier, 1, device_id={"box": high}, device_id_type=mesh)
    arrivals = n - 1 if swaps else 0
    if halos:
        arrivals = arrivals + has_low.astype(jnp.int32) + has_high.astype(jnp.int32)
    pl.semaphore_wait(barrier, arrivals)
    copies, locals_, ups, downs = [], [], [], []
    for j in range(halos):
        x, y = xs[swaps + j], ys[swaps + j]
        up = pltpu.make_async_remote_copy(
            x, y.at[0], halo_send.at[j, 0], halo_recv.at[j, 0],
            device_id={"box": high}, device_id_type=mesh)
        down = pltpu.make_async_remote_copy(
            x, y.at[2], halo_send.at[j, 1], halo_recv.at[j, 1],
            device_id={"box": low}, device_id_type=mesh)
        pl.when(has_high)(up.start)
        pl.when(has_low)(down.start)
        ups.append(up)
        downs.append(down)
    for d in [2, 1, 3] if n == 4 else range(1, n):
        for j in range(swaps):
            peer = lax.rem(me + d, n)
            copy = pltpu.make_async_remote_copy(
                xs[j].at[peer // shares[j]], ys[j].at[me], send.at[j, d], recv.at[j, d],
                device_id={"samp": peer}, device_id_type=mesh)
            copy.start()
            copies.append(copy)
    for j in range(count):
        if j < swaps:
            copy = pltpu.make_async_copy(xs[j].at[me // shares[j]], ys[j].at[me], own.at[j])
        else:
            copy = pltpu.make_async_copy(xs[j], ys[j].at[1], own.at[j])
        copy.start()
        locals_.append(copy)
    for copy in locals_ + copies:
        copy.wait()
    for up, down in zip(ups, downs):
        pl.when(has_high)(up.wait_send)
        pl.when(has_low)(down.wait_send)
        pl.when(has_low)(up.wait_recv)
        pl.when(has_high)(down.wait_recv)


def exchange(number, swaps, halos):
    n, runs = lax.axis_size("samp"), lax.axis_size("box")
    arrays = [x for x, _ in swaps] + list(halos)
    shapes = [jax.ShapeDtypeStruct((n,) + x.shape[1:], x.dtype) for x, _ in swaps]
    shapes += [jax.ShapeDtypeStruct((3,) + x.shape, x.dtype) for x in halos]
    dma = pltpu.SemaphoreType.DMA
    return pl.pallas_call(
        functools.partial(
            exchange_kernel, n, runs, len(swaps), len(halos), tuple(s for _, s in swaps)),
        in_specs=[pl.BlockSpec(memory_space=pl.ANY)] * len(arrays),
        out_specs=[pl.BlockSpec(memory_space=pl.ANY)] * len(arrays),
        out_shape=shapes,
        scratch_shapes=[
            dma((max(len(swaps), 1), n)),
            dma((max(len(swaps), 1), n)),
            dma((len(arrays),)),
            dma((max(len(halos), 1), 2)),
            dma((max(len(halos), 1), 2)),
        ],
        compiler_params=pltpu.CompilerParams(
            collective_id=number, has_side_effects=True, vmem_limit_bytes=VMEM_LIMIT),
    )(*arrays)


def ranks(key):
    count = key.shape[0]
    ids = jnp.arange(count, dtype=jnp.int32)
    before = (key[None, :] < key[:, None]) | (
        (key[None, :] == key[:, None]) & (ids[None, :] < ids[:, None]))
    rank = jnp.sum(before.astype(jnp.int32), axis=1)
    order = jnp.sum(jnp.where(rank[None, :] == ids[:, None], ids[None, :], 0), axis=1)
    return rank, order


def pick(values, index):
    hot = index[:, None] == jnp.arange(values.shape[0], dtype=jnp.int32)[None, :]
    return jnp.sum(jnp.where(hot, values[None, :], 0), axis=1)


def body(
    radiation, theta_mid, phi_mid, theta_top, phi_top, shift_mid, shift_top,
    octant_low, octant_mid, parent_low, parent_mid, trans_low, trans_mid, trans_top,
    far_low, far_mid, far_top, offset_low, offset_mid, offset_top,
):
    n = lax.axis_size("samp")
    me, box = lax.axis_index("samp"), lax.axis_index("box")
    lows, mids = octant_low.shape[0], octant_mid.shape[0]
    tops = mids // 4
    low_each, mid_each = lows // n, mids // n
    _, _, rows_low, p_low = radiation.shape
    rank_mid, order_mid = ranks(parent_mid)
    rank_low, order_low = ranks(pick(rank_mid, parent_low - box * mids))
    oct_low = lax.dynamic_slice_in_dim(pick(octant_low, order_low), me * low_each, low_each)
    oct_mid = lax.dynamic_slice_in_dim(pick(octant_mid, order_mid), me * mid_each, mid_each)

    grouped = jnp.take(radiation, order_low, axis=1)
    grouped = jnp.moveaxis(grouped.reshape(2, n, low_each, rows_low, p_low), 1, 0)
    low_parts, near_low = exchange(0, [(grouped, 1)], [radiation])
    mid_parts = go_up(low_parts, theta_mid, phi_mid, shift_mid, oct_low, mid_each)
    mid_rows, = exchange(1, [(mid_parts, 1)], [])
    top_parts = go_up(mid_parts, theta_top, phi_top, shift_top, oct_mid, 1)
    top_here, mid_here = middle_stage(
        2, mid_rows, top_parts, rank_mid, trans_mid, trans_top,
        entries(far_mid, mids)[order_mid], offset_mid[order_mid],
        entries(far_top, tops), offset_top)
    mid_in = go_down(top_here, theta_top, phi_top, shift_top, oct_mid, mid_here)
    low_in = go_down(mid_in, theta_mid, phi_mid, shift_mid, oct_low, None)
    return last_stage(
        3, low_in, near_low, trans_low, entries(far_low, lows), offset_low, rank_low)


def solution(mesh):
    in_specs = (
        P(None, "box", "samp", None),
        P(), P(), P(), P(), P(), P(),
        P("box"), P("box"), P("box"), P("box"),
        P(None, None, "samp", None),
        P(None, None, "samp", None),
        P(None, None, "samp", None),
        P("box", None), P("box", None), P("box", None),
        P("box", None), P("box", None), P("box", None),
    )
    out_specs = P(None, "box", "samp", None)
    return jax.shard_map(body, mesh=mesh, in_specs=in_specs, out_specs=out_specs, check_vma=False)
```

```python
import functools

import jax
import jax.numpy as jnp
from jax import lax
from jax.experimental import pallas as pl
from jax.experimental.pallas import tpu as pltpu
from jax.sharding import PartitionSpec as P

MIB = 1024 * 1024
VMEM = pltpu.VMEM
SMEM = pltpu.SMEM


def sincos(angle):
    half = 0.5 * angle
    z = half * half
    s = jnp.float32(1.0 / 6227020800.0)
    for c in (-1.0 / 39916800.0, 1.0 / 362880.0, -1.0 / 5040.0, 1.0 / 120.0, -1.0 / 6.0, 1.0):
        s = s * z + c
    s = s * half
    k = jnp.float32(1.0 / 479001600.0)
    for c in (-1.0 / 3628800.0, 1.0 / 40320.0, -1.0 / 720.0, 1.0 / 24.0, -0.5, 1.0):
        k = k * z + c
    return 2.0 * s * k, 1.0 - 2.0 * s * s


def split(x):
    high = x.astype(jnp.bfloat16)
    return high, (x - high.astype(jnp.float32)).astype(jnp.bfloat16)


def dot3(a, b):
    (ah, al), (bh, bl) = split(a), split(b)
    dot = functools.partial(jnp.dot, preferred_element_type=jnp.float32)
    return dot(ah, bl) + dot(al, bh) + dot(ah, bh)


def up_kernel(n, kids, oct_ref, x_ref, q_ref, rt_ref, shift_ref, out_ref, x_all, mixed):
    i = pl.program_id(0)
    rows = x_ref.shape[3]
    theta = n * rows
    rows_out = out_ref.shape[3]
    for r in range(2):
        for k in range(n):
            x_all[r * theta + k * rows:r * theta + (k + 1) * rows, :] = x_ref[k, r, 0]
    interp = dot3(x_all[...], rt_ref[...])
    q = q_ref[...]
    real = dot3(q, interp[:theta])
    imag = dot3(q, interp[theta:])
    sine, cosine = sincos(shift_ref[0])
    turned = (real * cosine - imag * sine, real * sine + imag * cosine)
    child = lax.rem(i, kids)

    @pl.when(child == 0)
    def _():
        for r in range(2):
            mixed[r] = turned[r]

    @pl.when(child > 0)
    def _():
        for r in range(2):
            mixed[r] = mixed[r] + turned[r]

    @pl.when(child == kids - 1)
    def _():
        for r in range(2):
            for k in range(n):
                out_ref[k, r, 0] = mixed[r, k * rows_out:(k + 1) * rows_out, :]


def go_up(x, theta_w, phi_w, angles, octant, parents):
    n, _, boxes, rows, p = x.shape
    s, q = theta_w.shape[0], phi_w.shape[0]
    kids = boxes // parents
    spec = pltpu.PrefetchScalarGridSpec(
        num_scalar_prefetch=1,
        grid=(boxes,),
        in_specs=[
            pl.BlockSpec((n, 2, 1, rows, p), lambda i, o: (0, 0, i, 0, 0)),
            pl.BlockSpec((s, n * rows), lambda i, o: (0, 0)),
            pl.BlockSpec((p, q), lambda i, o: (0, 0)),
            pl.BlockSpec((1, s, q), lambda i, o: (o[i], 0, 0)),
        ],
        out_specs=pl.BlockSpec((n, 2, 1, s // n, q), lambda i, o: (0, 0, i // kids, 0, 0)),
        scratch_shapes=[
            pltpu.VMEM((2 * n * rows, p), jnp.float32),
            pltpu.VMEM((2, s, q), jnp.float32),
        ],
    )
    return pl.pallas_call(
        functools.partial(up_kernel, n, kids),
        grid_spec=spec,
        out_shape=jax.ShapeDtypeStruct((n, 2, parents, s // n, q), jnp.float32),
        compiler_params=pltpu.CompilerParams(vmem_limit_bytes=24 * MIB),
    )(octant, x, theta_w, phi_w.T, angles)


def down_kernel(n, kids, with_add, oct_ref, g_ref, qt_ref, r_ref, shift_ref, *rest):
    if with_add:
        add_ref, out_ref, held, mixed, final = rest
    else:
        out_ref, held, mixed, final = rest
    i = pl.program_id(0)
    rows = g_ref.shape[3]
    theta = qt_ref.shape[0]
    rows_out = theta // n

    @pl.when(lax.rem(i, kids) == 0)
    def _():
        for r in range(2):
            for k in range(n):
                held[r, k * rows:(k + 1) * rows, :] = g_ref[k, r, 0]

    sine, cosine = sincos(shift_ref[0])
    real, imag = held[0], held[1]
    qt = qt_ref[...]
    mixed[:theta, :] = dot3(qt, real * cosine + imag * sine)
    mixed[theta:, :] = dot3(qt, imag * cosine - real * sine)
    final[...] = dot3(mixed[...], r_ref[...])
    for r in range(2):
        for k in range(n):
            part = final[r * theta + k * rows_out:r * theta + (k + 1) * rows_out, :]
            out_ref[k, r, 0] = part + add_ref[k, r, 0] if with_add else part


def go_down(g, theta_w, phi_w, angles, octant, add):
    n, _, parents, rows, q = g.shape
    boxes = octant.shape[0]
    kids = boxes // parents
    s, t = theta_w.shape
    p = phi_w.shape[1]
    block_out = pl.BlockSpec((n, 2, 1, t // n, p), lambda i, o: (0, 0, i, 0, 0))
    with_add = add is not None
    spec = pltpu.PrefetchScalarGridSpec(
        num_scalar_prefetch=1,
        grid=(boxes,),
        in_specs=[
            pl.BlockSpec((n, 2, 1, rows, q), lambda i, o: (0, 0, i // kids, 0, 0)),
            pl.BlockSpec((t, s), lambda i, o: (0, 0)),
            pl.BlockSpec((q, p), lambda i, o: (0, 0)),
            pl.BlockSpec((1, s, q), lambda i, o: (o[i], 0, 0)),
        ] + ([block_out] if with_add else []),
        out_specs=block_out,
        scratch_shapes=[
            pltpu.VMEM((2, s, q), jnp.float32),
            pltpu.VMEM((2 * t, q), jnp.float32),
            pltpu.VMEM((2 * t, p), jnp.float32),
        ],
    )
    args = (octant, g, theta_w.T, phi_w, angles) + ((add,) if with_add else ())
    return pl.pallas_call(
        functools.partial(down_kernel, n, kids, with_add),
        grid_spec=spec,
        out_shape=jax.ShapeDtypeStruct((n, 2, boxes, t // n, p), jnp.float32),
        compiler_params=pltpu.CompilerParams(vmem_limit_bytes=24 * MIB),
    )(*args)


def sum_far(boxes, noff, chunk, b, e_ref, o_ref, pat, tab, store):
    rows = pat.shape[1]
    for lo in range(0, rows, chunk):
        here = slice(lo, min(lo + chunk, rows))
        real = imag = None
        for f in range(e_ref.shape[1]):
            e, o = e_ref[b, f], o_ref[b, f]
            sr, si = pat[e, here, :], pat[e + boxes, here, :]
            cr, ci = tab[o, here, :], tab[o + noff, here, :]
            dr, di = sr * cr - si * ci, sr * ci + si * cr
            real = dr if real is None else real + dr
            imag = di if imag is None else imag + di
        store(here, real, imag)


def chunk_of(p):
    return 24 if p <= 256 else 16 if p <= 384 else 8


def entries(far_ids, boxes):
    local = far_ids - (lax.axis_index("box") - 1) * boxes
    return (local // boxes) * (2 * boxes) + local % boxes


MESH = pl.DeviceIdType.MESH


def peers_of(n):
    me = lax.axis_index("samp")
    return [(d, lax.rem(me + d, n)) for d in ([2, 1, 3] if n == 4 else range(1, n))]


def greet(n, runs, halos):
    barrier = pltpu.get_barrier_semaphore()
    for _, peer in peers_of(n):
        pl.semaphore_signal(barrier, 1, device_id={"samp": peer}, device_id_type=MESH)
    arrivals = n - 1
    if halos:
        box = lax.axis_index("box")
        has_low, has_high = box > 0, box < runs - 1

        @pl.when(has_low)
        def _():
            pl.semaphore_signal(barrier, 1, device_id={"box": box - 1}, device_id_type=MESH)

        @pl.when(has_high)
        def _():
            pl.semaphore_signal(barrier, 1, device_id={"box": box + 1}, device_id_type=MESH)

        arrivals = arrivals + has_low.astype(jnp.int32) + has_high.astype(jnp.int32)
    pl.semaphore_wait(barrier, arrivals)


def halo_copies(runs, near, size, send, recv):
    box = lax.axis_index("box")
    has_low, has_high = box > 0, box < runs - 1
    own = near.at[pl.ds(size, size)]
    up = pltpu.make_async_remote_copy(
        own, near.at[pl.ds(0, size)], send.at[0], recv.at[0],
        device_id={"box": jnp.minimum(box + 1, runs - 1)}, device_id_type=MESH)
    down = pltpu.make_async_remote_copy(
        own, near.at[pl.ds(2 * size, size)], send.at[1], recv.at[1],
        device_id={"box": jnp.maximum(box - 1, 0)}, device_id_type=MESH)

    def start():
        pl.when(has_high)(up.start)
        pl.when(has_low)(down.start)

    def arrive():
        pl.when(has_low)(up.wait_recv)
        pl.when(has_high)(down.wait_recv)

    def leave():
        pl.when(has_high)(up.wait_send)
        pl.when(has_low)(down.wait_send)

    return start, arrive, leave


def middle_kernel(
    n, runs, e_mid, o_mid, rank, e_top, o_top, octant, mid_parts, tab_mid, tab_top,
    theta, phi_t, angles, top_here, mid_here, near_mid, near_top, top_rows, in_mid, in_top,
    mid_rows, top_parts, x_all, mixed, send, recv, halo_send, halo_recv,
):
    me = lax.axis_index("samp")
    mids, tops = e_mid.shape[0], e_top.shape[0]
    each, share = mids // n, n // tops
    noff = tab_mid.shape[0] // 2
    greet(n, runs, True)

    def swap(j, src, dst, share):
        copies = [
            pltpu.make_async_remote_copy(
                src.at[peer // share], dst.at[me], send.at[j, d], recv.at[j, d],
                device_id={"samp": peer}, device_id_type=MESH)
            for d, peer in peers_of(n)
        ]
        for copy in copies:
            copy.start()
        return copies

    mids_up = swap(3, mid_parts, mid_rows, 1)
    mid_rows[me] = mid_parts[me]
    rows, rows_top = mid_parts.shape[3], top_parts.shape[3]
    full = n * rows
    for i in range(each):
        for r in range(2):
            for k in range(n):
                x_all[r * full + k * rows:r * full + (k + 1) * rows, :] = mid_parts[k, r, i]
        interp = dot3(x_all[...], phi_t[...])
        real = dot3(theta[...], interp[:full])
        imag = dot3(theta[...], interp[full:])
        sine, cosine = sincos(angles[octant[i]])
        turned = (real * cosine - imag * sine, real * sine + imag * cosine)
        for r in range(2):
            mixed[r] = turned[r] if i == 0 else mixed[r] + turned[r]
    for r in range(2):
        for k in range(n):
            top_parts[k, r, 0] = mixed[r, k * rows_top:(k + 1) * rows_top, :]
    tops_out = swap(0, top_parts, top_rows, 1)
    for copy in mids_up:
        copy.wait()

    def natural(b, carry):
        place = rank[b]
        for r in range(2):
            near_mid[(2 + r) * mids + b] = mid_rows[place // each, r, lax.rem(place, each)]
        return carry

    lax.fori_loop(0, mids, natural, 0)
    start_mid, mid_arrives, mid_leaves = halo_copies(
        runs, near_mid, 2 * mids, halo_send.at[0], halo_recv.at[0])
    start_mid()
    top_rows[me] = top_parts[me]
    mid_arrives()

    def far_mid(b, carry):
        def store(here, real, imag):
            in_mid[b // each, 0, lax.rem(b, each), here, :] = real
            in_mid[b // each, 1, lax.rem(b, each), here, :] = imag

        sum_far(mids, noff, chunk_of(tab_mid.shape[2]), b, e_mid, o_mid, near_mid, tab_mid, store)
        return carry

    lax.fori_loop(0, mids, far_mid, 0)
    for copy in tops_out:
        copy.wait()
    mids_out = swap(1, in_mid, mid_here, 1)
    mid_here[me] = in_mid[me]
    for t in range(tops):
        for r in range(2):
            total = top_rows[t * share, r, 0]
            for k in range(1, share):
                total = total + top_rows[t * share + k, r, 0]
            near_top[(2 + r) * tops + t] = total
    start_top, top_arrives, top_leaves = halo_copies(
        runs, near_top, 2 * tops, halo_send.at[1], halo_recv.at[1])
    start_top()
    top_arrives()

    def far_top(b, carry):
        def store(here, real, imag):
            in_top[b, 0, 0, here, :] = real
            in_top[b, 1, 0, here, :] = imag

        sum_far(tops, noff, chunk_of(tab_top.shape[2]), b, e_top, o_top, near_top, tab_top, store)
        return carry

    lax.fori_loop(0, tops, far_top, 0)
    tops_back = swap(2, in_top, top_here, share)
    top_here[me] = in_top[me // share]
    for copy in mids_out + tops_back:
        copy.wait()
    mid_leaves()
    top_leaves()


def flat(x, lead):
    return x.reshape((-1,) + x.shape[lead:])


def middle_stage(
    number, mid_parts, octant, theta_w, phi_w, angles, rank, trans_mid, trans_top,
    e_mid, o_mid, e_top, o_top,
):
    n, runs = lax.axis_size("samp"), lax.axis_size("box")
    mids, tops = e_mid.shape[0], e_top.shape[0]
    f32, dma = jnp.float32, pltpu.SemaphoreType.DMA
    s, q = theta_w.shape[0], phi_w.shape[0]
    row_mid, row_top = mid_parts.shape[3:], (s // n, q)
    top_shape = (n, 2, 1) + row_top
    spec = pl.BlockSpec(memory_space=VMEM)
    return pl.pallas_call(
        functools.partial(middle_kernel, n, runs),
        in_specs=[pl.BlockSpec(memory_space=SMEM)] * 6 + [spec] * 6,
        out_specs=[spec, spec],
        out_shape=[
            jax.ShapeDtypeStruct(top_shape, f32),
            jax.ShapeDtypeStruct(mid_parts.shape, f32),
        ],
        scratch_shapes=[
            pltpu.VMEM((6 * mids,) + row_mid, f32),
            pltpu.VMEM((6 * tops,) + row_top, f32),
            pltpu.VMEM(top_shape, f32),
            pltpu.VMEM(mid_parts.shape, f32),
            pltpu.VMEM((tops, 2, 1) + row_top, f32),
            pltpu.VMEM(mid_parts.shape, f32),
            pltpu.VMEM(top_shape, f32),
            pltpu.VMEM((2 * theta_w.shape[1], phi_w.shape[1]), f32),
            pltpu.VMEM((2, s, q), f32),
            dma((4, n)), dma((4, n)), dma((2, 2)), dma((2, 2)),
        ],
        compiler_params=pltpu.CompilerParams(
            collective_id=number, has_side_effects=True, vmem_limit_bytes=40 * MIB),
    )(
        e_mid, o_mid, rank, e_top, o_top, octant, mid_parts, flat(trans_mid, 2),
        flat(trans_top, 2), theta_w, phi_w.T, angles)


def last_kernel(n, runs, e_ref, o_ref, at_ref, low_in, pat, tab, out_ref, landed, send, recv):
    me = lax.axis_index("samp")
    boxes = e_ref.shape[0]
    size = low_in.shape[0] // n
    noff = tab.shape[0] // 2
    greet(n, runs, False)
    copies = [
        pltpu.make_async_remote_copy(
            low_in.at[pl.ds(peer * size, size)], landed.at[pl.ds(me * size, size)],
            send.at[d], recv.at[d], device_id={"samp": peer}, device_id_type=MESH)
        for d, peer in peers_of(n)
    ]
    for copy in copies:
        copy.start()
    landed[pl.ds(me * size, size)] = low_in[pl.ds(me * size, size)]

    def far(b, carry):
        def store(here, real, imag):
            out_ref[b, here, :] = real
            out_ref[b + boxes, here, :] = imag

        sum_far(boxes, noff, chunk_of(tab.shape[2]), b, e_ref, o_ref, pat, tab, store)
        return carry

    lax.fori_loop(0, boxes, far, 0)
    for copy in copies:
        copy.wait()

    def add(b, carry):
        place = at_ref[b]
        out_ref[b] = out_ref[b] + landed[place]
        out_ref[b + boxes] = out_ref[b + boxes] + landed[place + size // 2]
        return carry

    lax.fori_loop(0, boxes, add, 0)


def last_stage(number, low_in, near, table, e_low, o_low, rank):
    n, runs = lax.axis_size("samp"), lax.axis_size("box")
    boxes, each = e_low.shape[0], low_in.shape[2]
    row = low_in.shape[3:]
    place = (rank // each) * (2 * each) + rank % each
    dma = pltpu.SemaphoreType.DMA
    spec = pl.BlockSpec(memory_space=VMEM)
    return pl.pallas_call(
        functools.partial(last_kernel, n, runs),
        in_specs=[pl.BlockSpec(memory_space=SMEM)] * 3 + [spec] * 3,
        out_specs=spec,
        out_shape=jax.ShapeDtypeStruct((2 * boxes,) + row, jnp.float32),
        scratch_shapes=[pltpu.VMEM((2 * boxes,) + row, jnp.float32), dma((n,)), dma((n,))],
        compiler_params=pltpu.CompilerParams(
            collective_id=number, has_side_effects=True, vmem_limit_bytes=32 * MIB),
    )(e_low, o_low, place, flat(low_in, 3), flat(near, 3), flat(table, 2)).reshape((2, boxes) + row)


def exchange_kernel(n, runs, swaps, halos, shares, *refs):
    count = swaps + halos
    xs, ys = refs[:count], refs[count:2 * count]
    send, recv, own, halo_send, halo_recv = refs[2 * count:]
    me = lax.axis_index("samp")
    box = lax.axis_index("box")
    barrier = pltpu.get_barrier_semaphore()
    has_low, has_high = box > 0, box < runs - 1
    low, high = jnp.maximum(box - 1, 0), jnp.minimum(box + 1, runs - 1)
    mesh = pl.DeviceIdType.MESH
    if swaps:
        for d in range(1, n):
            peer = lax.rem(me + d, n)
            pl.semaphore_signal(barrier, 1, device_id={"samp": peer}, device_id_type=mesh)
    if halos:
        @pl.when(has_low)
        def _():
            pl.semaphore_signal(barrier, 1, device_id={"box": low}, device_id_type=mesh)

        @pl.when(has_high)
        def _():
            pl.semaphore_signal(barrier, 1, device_id={"box": high}, device_id_type=mesh)
    arrivals = n - 1 if swaps else 0
    if halos:
        arrivals = arrivals + has_low.astype(jnp.int32) + has_high.astype(jnp.int32)
    pl.semaphore_wait(barrier, arrivals)
    copies, locals_, ups, downs = [], [], [], []
    for j in range(halos):
        x, y = xs[swaps + j], ys[swaps + j]
        up = pltpu.make_async_remote_copy(
            x, y.at[0], halo_send.at[j, 0], halo_recv.at[j, 0],
            device_id={"box": high}, device_id_type=mesh)
        down = pltpu.make_async_remote_copy(
            x, y.at[2], halo_send.at[j, 1], halo_recv.at[j, 1],
            device_id={"box": low}, device_id_type=mesh)
        pl.when(has_high)(up.start)
        pl.when(has_low)(down.start)
        ups.append(up)
        downs.append(down)
    for d in [2, 1, 3] if n == 4 else range(1, n):
        for j in range(swaps):
            peer = lax.rem(me + d, n)
            copy = pltpu.make_async_remote_copy(
                xs[j].at[peer // shares[j]], ys[j].at[me], send.at[j, d], recv.at[j, d],
                device_id={"samp": peer}, device_id_type=mesh)
            copy.start()
            copies.append(copy)
    for j in range(count):
        if j < swaps:
            copy = pltpu.make_async_copy(xs[j].at[me // shares[j]], ys[j].at[me], own.at[j])
        else:
            copy = pltpu.make_async_copy(xs[j], ys[j].at[1], own.at[j])
        copy.start()
        locals_.append(copy)
    for copy in locals_ + copies:
        copy.wait()
    for up, down in zip(ups, downs):
        pl.when(has_high)(up.wait_send)
        pl.when(has_low)(down.wait_send)
        pl.when(has_low)(up.wait_recv)
        pl.when(has_high)(down.wait_recv)


def exchange(number, swaps, halos):
    n, runs = lax.axis_size("samp"), lax.axis_size("box")
    arrays = [x for x, _ in swaps] + list(halos)
    shapes = [jax.ShapeDtypeStruct((n,) + x.shape[1:], x.dtype) for x, _ in swaps]
    shapes += [jax.ShapeDtypeStruct((3,) + x.shape, x.dtype) for x in halos]
    dma = pltpu.SemaphoreType.DMA
    return pl.pallas_call(
        functools.partial(
            exchange_kernel, n, runs, len(swaps), len(halos), tuple(s for _, s in swaps)),
        in_specs=[pl.BlockSpec(memory_space=pl.ANY)] * len(arrays),
        out_specs=[pl.BlockSpec(memory_space=pl.ANY)] * len(arrays),
        out_shape=shapes,
        scratch_shapes=[
            dma((max(len(swaps), 1), n)),
            dma((max(len(swaps), 1), n)),
            dma((len(arrays),)),
            dma((max(len(halos), 1), 2)),
            dma((max(len(halos), 1), 2)),
        ],
        compiler_params=pltpu.CompilerParams(
            collective_id=number, has_side_effects=True, vmem_limit_bytes=8 * MIB),
    )(*arrays)


def ranks(key):
    count = key.shape[0]
    ids = jnp.arange(count, dtype=jnp.int32)
    before = (key[None, :] < key[:, None]) | (
        (key[None, :] == key[:, None]) & (ids[None, :] < ids[:, None]))
    rank = jnp.sum(before.astype(jnp.int32), axis=1)
    order = jnp.sum(jnp.where(rank[None, :] == ids[:, None], ids[None, :], 0), axis=1)
    return rank, order


def pick(values, index):
    hot = index[:, None] == jnp.arange(values.shape[0], dtype=jnp.int32)[None, :]
    return jnp.sum(jnp.where(hot, values[None, :], 0), axis=1)


def body(
    radiation, theta_mid, phi_mid, theta_top, phi_top, shift_mid, shift_top,
    octant_low, octant_mid, parent_low, parent_mid, trans_low, trans_mid, trans_top,
    far_low, far_mid, far_top, offset_low, offset_mid, offset_top,
):
    n = lax.axis_size("samp")
    me, box = lax.axis_index("samp"), lax.axis_index("box")
    lows, mids = octant_low.shape[0], octant_mid.shape[0]
    tops = mids // 4
    low_each, mid_each = lows // n, mids // n
    _, _, rows_low, p_low = radiation.shape
    rank_mid, order_mid = ranks(parent_mid)
    rank_low, order_low = ranks(pick(rank_mid, parent_low - box * mids))
    oct_low = lax.dynamic_slice_in_dim(pick(octant_low, order_low), me * low_each, low_each)
    oct_mid = lax.dynamic_slice_in_dim(pick(octant_mid, order_mid), me * mid_each, mid_each)

    grouped = jnp.take(radiation, order_low, axis=1)
    grouped = jnp.moveaxis(grouped.reshape(2, n, low_each, rows_low, p_low), 1, 0)
    low_parts, near_low = exchange(0, [(grouped, 1)], [radiation])
    mid_parts = go_up(low_parts, theta_mid, phi_mid, shift_mid, oct_low, mid_each)
    top_here, mid_here = middle_stage(
        2, mid_parts, oct_mid, theta_top, phi_top, shift_top, rank_mid, trans_mid, trans_top,
        entries(far_mid, mids)[order_mid], offset_mid[order_mid],
        entries(far_top, tops), offset_top)
    mid_in = go_down(top_here, theta_top, phi_top, shift_top, oct_mid, mid_here)
    low_in = go_down(mid_in, theta_mid, phi_mid, shift_mid, oct_low, None)
    return last_stage(
        3, low_in, near_low, trans_low, entries(far_low, lows), offset_low, rank_low)


def solution(mesh):
    in_specs = (
        P(None, "box", "samp", None),
        P(), P(), P(), P(), P(), P(),
        P("box"), P("box"), P("box"), P("box"),
        P(None, None, "samp", None),
        P(None, None, "samp", None),
        P(None, None, "samp", None),
        P("box", None), P("box", None), P("box", None),
        P("box", None), P("box", None), P("box", None),
    )
    out_specs = P(None, "box", "samp", None)
    return jax.shard_map(body, mesh=mesh, in_specs=in_specs, out_specs=out_specs, check_vma=False)
```

```python
import functools

import jax
import jax.numpy as jnp
from jax import lax
from jax.experimental import pallas as pl
from jax.experimental.pallas import tpu as pltpu
from jax.sharding import PartitionSpec as P

GRANT = 60 * 1024 * 1024
VMEM = pltpu.VMEM
SMEM = pltpu.SMEM


def sincos(angle):
    half = 0.5 * angle
    z = half * half
    s = jnp.float32(1.0 / 6227020800.0)
    for c in (-1.0 / 39916800.0, 1.0 / 362880.0, -1.0 / 5040.0, 1.0 / 120.0, -1.0 / 6.0, 1.0):
        s = s * z + c
    s = s * half
    k = jnp.float32(1.0 / 479001600.0)
    for c in (-1.0 / 3628800.0, 1.0 / 40320.0, -1.0 / 720.0, 1.0 / 24.0, -0.5, 1.0):
        k = k * z + c
    return 2.0 * s * k, 1.0 - 2.0 * s * s


def split(x):
    high = x.astype(jnp.bfloat16)
    return high, (x - high.astype(jnp.float32)).astype(jnp.bfloat16)


def dot3(a, b):
    (ah, al), (bh, bl) = split(a), split(b)
    dot = functools.partial(jnp.dot, preferred_element_type=jnp.float32)
    return dot(ah, bl) + dot(al, bh) + dot(ah, bh)


def up_kernel(n, kids, oct_ref, x_ref, q_ref, rt_ref, shift_ref, out_ref, x_all, mixed):
    i = pl.program_id(0)
    rows = x_ref.shape[3]
    theta = n * rows
    rows_out = out_ref.shape[3]
    for r in range(2):
        for k in range(n):
            x_all[r * theta + k * rows:r * theta + (k + 1) * rows, :] = x_ref[k, r, 0]
    interp = dot3(x_all[...], rt_ref[...])
    q = q_ref[...]
    real = dot3(q, interp[:theta])
    imag = dot3(q, interp[theta:])
    sine, cosine = sincos(shift_ref[0])
    turned = (real * cosine - imag * sine, real * sine + imag * cosine)
    child = lax.rem(i, kids)

    @pl.when(child == 0)
    def _():
        for r in range(2):
            mixed[r] = turned[r]

    @pl.when(child > 0)
    def _():
        for r in range(2):
            mixed[r] = mixed[r] + turned[r]

    @pl.when(child == kids - 1)
    def _():
        for r in range(2):
            for k in range(n):
                out_ref[k, r, 0] = mixed[r, k * rows_out:(k + 1) * rows_out, :]


def go_up(x, theta_w, phi_w, angles, octant, parents):
    n, _, boxes, rows, p = x.shape
    s, q = theta_w.shape[0], phi_w.shape[0]
    kids = boxes // parents
    spec = pltpu.PrefetchScalarGridSpec(
        num_scalar_prefetch=1,
        grid=(boxes,),
        in_specs=[
            pl.BlockSpec((n, 2, 1, rows, p), lambda i, o: (0, 0, i, 0, 0)),
            pl.BlockSpec((s, n * rows), lambda i, o: (0, 0)),
            pl.BlockSpec((p, q), lambda i, o: (0, 0)),
            pl.BlockSpec((1, s, q), lambda i, o: (o[i], 0, 0)),
        ],
        out_specs=pl.BlockSpec((n, 2, 1, s // n, q), lambda i, o: (0, 0, i // kids, 0, 0)),
        scratch_shapes=[
            pltpu.VMEM((2 * n * rows, p), jnp.float32),
            pltpu.VMEM((2, s, q), jnp.float32),
        ],
    )
    return pl.pallas_call(
        functools.partial(up_kernel, n, kids),
        grid_spec=spec,
        out_shape=jax.ShapeDtypeStruct((n, 2, parents, s // n, q), jnp.float32),
        compiler_params=pltpu.CompilerParams(vmem_limit_bytes=GRANT),
    )(octant, x, theta_w, phi_w.T, angles)


def down_kernel(n, kids, with_add, oct_ref, g_ref, qt_ref, r_ref, shift_ref, *rest):
    if with_add:
        add_ref, out_ref, held, mixed, final = rest
    else:
        out_ref, held, mixed, final = rest
    i = pl.program_id(0)
    rows = g_ref.shape[3]
    theta = qt_ref.shape[0]
    rows_out = theta // n

    @pl.when(lax.rem(i, kids) == 0)
    def _():
        for r in range(2):
            for k in range(n):
                held[r, k * rows:(k + 1) * rows, :] = g_ref[k, r, 0]

    sine, cosine = sincos(shift_ref[0])
    real, imag = held[0], held[1]
    qt = qt_ref[...]
    mixed[:theta, :] = dot3(qt, real * cosine + imag * sine)
    mixed[theta:, :] = dot3(qt, imag * cosine - real * sine)
    final[...] = dot3(mixed[...], r_ref[...])
    for r in range(2):
        for k in range(n):
            part = final[r * theta + k * rows_out:r * theta + (k + 1) * rows_out, :]
            out_ref[k, r, 0] = part + add_ref[k, r, 0] if with_add else part


def go_down(g, theta_w, phi_w, angles, octant, add):
    n, _, parents, rows, q = g.shape
    boxes = octant.shape[0]
    kids = boxes // parents
    s, t = theta_w.shape
    p = phi_w.shape[1]
    block_out = pl.BlockSpec((n, 2, 1, t // n, p), lambda i, o: (0, 0, i, 0, 0))
    with_add = add is not None
    spec = pltpu.PrefetchScalarGridSpec(
        num_scalar_prefetch=1,
        grid=(boxes,),
        in_specs=[
            pl.BlockSpec((n, 2, 1, rows, q), lambda i, o: (0, 0, i // kids, 0, 0)),
            pl.BlockSpec((t, s), lambda i, o: (0, 0)),
            pl.BlockSpec((q, p), lambda i, o: (0, 0)),
            pl.BlockSpec((1, s, q), lambda i, o: (o[i], 0, 0)),
        ] + ([block_out] if with_add else []),
        out_specs=block_out,
        scratch_shapes=[
            pltpu.VMEM((2, s, q), jnp.float32),
            pltpu.VMEM((2 * t, q), jnp.float32),
            pltpu.VMEM((2 * t, p), jnp.float32),
        ],
    )
    args = (octant, g, theta_w.T, phi_w, angles) + ((add,) if with_add else ())
    return pl.pallas_call(
        functools.partial(down_kernel, n, kids, with_add),
        grid_spec=spec,
        out_shape=jax.ShapeDtypeStruct((n, 2, boxes, t // n, p), jnp.float32),
        compiler_params=pltpu.CompilerParams(vmem_limit_bytes=GRANT),
    )(*args)


def sum_far(boxes, noff, chunk, b, e_ref, o_ref, pat, tab, store):
    rows = pat.shape[1]
    for lo in range(0, rows, chunk):
        here = slice(lo, min(lo + chunk, rows))
        real = imag = None
        for f in range(e_ref.shape[1]):
            e, o = e_ref[b, f], o_ref[b, f]
            sr, si = pat[e, here, :], pat[e + boxes, here, :]
            cr, ci = tab[o, here, :], tab[o + noff, here, :]
            dr, di = sr * cr - si * ci, sr * ci + si * cr
            real = dr if real is None else real + dr
            imag = di if imag is None else imag + di
        store(here, real, imag)


def chunk_of(p):
    return 24 if p <= 256 else 16 if p <= 384 else 8


def entries(far_ids, boxes):
    local = far_ids - (lax.axis_index("box") - 1) * boxes
    return (local // boxes) * (2 * boxes) + local % boxes


MESH = pl.DeviceIdType.MESH


def peers_of(n):
    me = lax.axis_index("samp")
    return [(d, lax.rem(me + d, n)) for d in ([2, 1, 3] if n == 4 else range(1, n))]


def greet(n, runs, halos):
    barrier = pltpu.get_barrier_semaphore()
    for _, peer in peers_of(n):
        pl.semaphore_signal(barrier, 1, device_id={"samp": peer}, device_id_type=MESH)
    arrivals = n - 1
    if halos:
        box = lax.axis_index("box")
        has_low, has_high = box > 0, box < runs - 1

        @pl.when(has_low)
        def _():
            pl.semaphore_signal(barrier, 1, device_id={"box": box - 1}, device_id_type=MESH)

        @pl.when(has_high)
        def _():
            pl.semaphore_signal(barrier, 1, device_id={"box": box + 1}, device_id_type=MESH)

        arrivals = arrivals + has_low.astype(jnp.int32) + has_high.astype(jnp.int32)
    pl.semaphore_wait(barrier, arrivals)


def halo_copies(runs, near, size, send, recv):
    box = lax.axis_index("box")
    has_low, has_high = box > 0, box < runs - 1
    own = near.at[pl.ds(size, size)]
    up = pltpu.make_async_remote_copy(
        own, near.at[pl.ds(0, size)], send.at[0], recv.at[0],
        device_id={"box": jnp.minimum(box + 1, runs - 1)}, device_id_type=MESH)
    down = pltpu.make_async_remote_copy(
        own, near.at[pl.ds(2 * size, size)], send.at[1], recv.at[1],
        device_id={"box": jnp.maximum(box - 1, 0)}, device_id_type=MESH)

    def start():
        pl.when(has_high)(up.start)
        pl.when(has_low)(down.start)

    def arrive():
        pl.when(has_low)(up.wait_recv)
        pl.when(has_high)(down.wait_recv)

    def leave():
        pl.when(has_high)(up.wait_send)
        pl.when(has_low)(down.wait_send)

    return start, arrive, leave


def middle_kernel(
    n, runs, e_mid, o_mid, rank, e_top, o_top, octant, mid_parts, tab_mid, tab_top,
    theta, phi_t, angles, top_here, mid_here, near_mid, near_top, top_rows, in_mid, in_top,
    mid_rows, top_parts, x_all, mixed, send, recv, halo_send, halo_recv,
):
    me = lax.axis_index("samp")
    mids, tops = e_mid.shape[0], e_top.shape[0]
    each, share = mids // n, n // tops
    noff = tab_mid.shape[0] // 2
    greet(n, runs, True)

    def swap(j, src, dst, share):
        copies = [
            pltpu.make_async_remote_copy(
                src.at[peer // share], dst.at[me], send.at[j, d], recv.at[j, d],
                device_id={"samp": peer}, device_id_type=MESH)
            for d, peer in peers_of(n)
        ]
        for copy in copies:
            copy.start()
        return copies

    mids_up = swap(3, mid_parts, mid_rows, 1)
    mid_rows[me] = mid_parts[me]
    rows, rows_top = mid_parts.shape[3], top_parts.shape[3]
    full = n * rows
    for i in range(each):
        for r in range(2):
            for k in range(n):
                x_all[r * full + k * rows:r * full + (k + 1) * rows, :] = mid_parts[k, r, i]
        interp = dot3(x_all[...], phi_t[...])
        real = dot3(theta[...], interp[:full])
        imag = dot3(theta[...], interp[full:])
        sine, cosine = sincos(angles[octant[i]])
        turned = (real * cosine - imag * sine, real * sine + imag * cosine)
        for r in range(2):
            mixed[r] = turned[r] if i == 0 else mixed[r] + turned[r]
    for r in range(2):
        for k in range(n):
            top_parts[k, r, 0] = mixed[r, k * rows_top:(k + 1) * rows_top, :]
    tops_out = swap(0, top_parts, top_rows, 1)
    for copy in mids_up:
        copy.wait()

    def natural(b, carry):
        place = rank[b]
        for r in range(2):
            near_mid[(2 + r) * mids + b] = mid_rows[place // each, r, lax.rem(place, each)]
        return carry

    lax.fori_loop(0, mids, natural, 0)
    start_mid, mid_arrives, mid_leaves = halo_copies(
        runs, near_mid, 2 * mids, halo_send.at[0], halo_recv.at[0])
    start_mid()
    top_rows[me] = top_parts[me]
    mid_arrives()

    def far_mid(b, carry):
        def store(here, real, imag):
            in_mid[b // each, 0, lax.rem(b, each), here, :] = real
            in_mid[b // each, 1, lax.rem(b, each), here, :] = imag

        sum_far(mids, noff, chunk_of(tab_mid.shape[2]), b, e_mid, o_mid, near_mid, tab_mid, store)
        return carry

    lax.fori_loop(0, mids, far_mid, 0)
    for copy in tops_out:
        copy.wait()
    mids_out = swap(1, in_mid, mid_here, 1)
    mid_here[me] = in_mid[me]
    for t in range(tops):
        for r in range(2):
            total = top_rows[t * share, r, 0]
            for k in range(1, share):
                total = total + top_rows[t * share + k, r, 0]
            near_top[(2 + r) * tops + t] = total
    start_top, top_arrives, top_leaves = halo_copies(
        runs, near_top, 2 * tops, halo_send.at[1], halo_recv.at[1])
    start_top()
    top_arrives()

    def far_top(b, carry):
        def store(here, real, imag):
            in_top[b, 0, 0, here, :] = real
            in_top[b, 1, 0, here, :] = imag

        sum_far(tops, noff, chunk_of(tab_top.shape[2]), b, e_top, o_top, near_top, tab_top, store)
        return carry

    lax.fori_loop(0, tops, far_top, 0)
    tops_back = swap(2, in_top, top_here, share)
    top_here[me] = in_top[me // share]
    for copy in mids_out + tops_back:
        copy.wait()
    mid_leaves()
    top_leaves()


def flat(x, lead):
    return x.reshape((-1,) + x.shape[lead:])


def middle_stage(
    number, mid_parts, octant, theta_w, phi_w, angles, rank, trans_mid, trans_top,
    e_mid, o_mid, e_top, o_top,
):
    n, runs = lax.axis_size("samp"), lax.axis_size("box")
    mids, tops = e_mid.shape[0], e_top.shape[0]
    f32, dma = jnp.float32, pltpu.SemaphoreType.DMA
    s, q = theta_w.shape[0], phi_w.shape[0]
    row_mid, row_top = mid_parts.shape[3:], (s // n, q)
    top_shape = (n, 2, 1) + row_top
    spec = pl.BlockSpec(memory_space=VMEM)
    return pl.pallas_call(
        functools.partial(middle_kernel, n, runs),
        in_specs=[pl.BlockSpec(memory_space=SMEM)] * 6 + [spec] * 6,
        out_specs=[spec, spec],
        out_shape=[
            jax.ShapeDtypeStruct(top_shape, f32),
            jax.ShapeDtypeStruct(mid_parts.shape, f32),
        ],
        scratch_shapes=[
            pltpu.VMEM((6 * mids,) + row_mid, f32),
            pltpu.VMEM((6 * tops,) + row_top, f32),
            pltpu.VMEM(top_shape, f32),
            pltpu.VMEM(mid_parts.shape, f32),
            pltpu.VMEM((tops, 2, 1) + row_top, f32),
            pltpu.VMEM(mid_parts.shape, f32),
            pltpu.VMEM(top_shape, f32),
            pltpu.VMEM((2 * theta_w.shape[1], phi_w.shape[1]), f32),
            pltpu.VMEM((2, s, q), f32),
            dma((4, n)), dma((4, n)), dma((2, 2)), dma((2, 2)),
        ],
        compiler_params=pltpu.CompilerParams(
            collective_id=number, has_side_effects=True, vmem_limit_bytes=GRANT),
    )(
        e_mid, o_mid, rank, e_top, o_top, octant, mid_parts, flat(trans_mid, 2),
        flat(trans_top, 2), theta_w, phi_w.T, angles)


def last_kernel(n, runs, e_ref, o_ref, at_ref, low_in, pat, tab, out_ref, landed, send, recv):
    me = lax.axis_index("samp")
    boxes = e_ref.shape[0]
    size = low_in.shape[0] // n
    noff = tab.shape[0] // 2
    greet(n, runs, False)
    copies = [
        pltpu.make_async_remote_copy(
            low_in.at[pl.ds(peer * size, size)], landed.at[pl.ds(me * size, size)],
            send.at[d], recv.at[d], device_id={"samp": peer}, device_id_type=MESH)
        for d, peer in peers_of(n)
    ]
    for copy in copies:
        copy.start()
    landed[pl.ds(me * size, size)] = low_in[pl.ds(me * size, size)]

    def far(b, carry):
        def store(here, real, imag):
            out_ref[b, here, :] = real
            out_ref[b + boxes, here, :] = imag

        sum_far(boxes, noff, chunk_of(tab.shape[2]), b, e_ref, o_ref, pat, tab, store)
        return carry

    lax.fori_loop(0, boxes, far, 0)
    for copy in copies:
        copy.wait()

    def add(b, carry):
        place = at_ref[b]
        out_ref[b] = out_ref[b] + landed[place]
        out_ref[b + boxes] = out_ref[b + boxes] + landed[place + size // 2]
        return carry

    lax.fori_loop(0, boxes, add, 0)


def last_stage(number, low_in, near, table, e_low, o_low, rank):
    n, runs = lax.axis_size("samp"), lax.axis_size("box")
    boxes, each = e_low.shape[0], low_in.shape[2]
    row = low_in.shape[3:]
    place = (rank // each) * (2 * each) + rank % each
    dma = pltpu.SemaphoreType.DMA
    spec = pl.BlockSpec(memory_space=VMEM)
    return pl.pallas_call(
        functools.partial(last_kernel, n, runs),
        in_specs=[pl.BlockSpec(memory_space=SMEM)] * 3 + [spec] * 3,
        out_specs=spec,
        out_shape=jax.ShapeDtypeStruct((2 * boxes,) + row, jnp.float32),
        scratch_shapes=[pltpu.VMEM((2 * boxes,) + row, jnp.float32), dma((n,)), dma((n,))],
        compiler_params=pltpu.CompilerParams(
            collective_id=number, has_side_effects=True, vmem_limit_bytes=GRANT),
    )(e_low, o_low, place, flat(low_in, 3), flat(near, 3), flat(table, 2)).reshape((2, boxes) + row)


def exchange_kernel(n, runs, swaps, halos, shares, *refs):
    count = swaps + halos
    xs, ys = refs[:count], refs[count:2 * count]
    send, recv, own, halo_send, halo_recv = refs[2 * count:]
    me = lax.axis_index("samp")
    box = lax.axis_index("box")
    barrier = pltpu.get_barrier_semaphore()
    has_low, has_high = box > 0, box < runs - 1
    low, high = jnp.maximum(box - 1, 0), jnp.minimum(box + 1, runs - 1)
    mesh = pl.DeviceIdType.MESH
    if swaps:
        for d in range(1, n):
            peer = lax.rem(me + d, n)
            pl.semaphore_signal(barrier, 1, device_id={"samp": peer}, device_id_type=mesh)
    if halos:
        @pl.when(has_low)
        def _():
            pl.semaphore_signal(barrier, 1, device_id={"box": low}, device_id_type=mesh)

        @pl.when(has_high)
        def _():
            pl.semaphore_signal(barrier, 1, device_id={"box": high}, device_id_type=mesh)
    arrivals = n - 1 if swaps else 0
    if halos:
        arrivals = arrivals + has_low.astype(jnp.int32) + has_high.astype(jnp.int32)
    pl.semaphore_wait(barrier, arrivals)
    copies, locals_, ups, downs = [], [], [], []
    for j in range(halos):
        x, y = xs[swaps + j], ys[swaps + j]
        up = pltpu.make_async_remote_copy(
            x, y.at[0], halo_send.at[j, 0], halo_recv.at[j, 0],
            device_id={"box": high}, device_id_type=mesh)
        down = pltpu.make_async_remote_copy(
            x, y.at[2], halo_send.at[j, 1], halo_recv.at[j, 1],
            device_id={"box": low}, device_id_type=mesh)
        pl.when(has_high)(up.start)
        pl.when(has_low)(down.start)
        ups.append(up)
        downs.append(down)
    for d in [2, 1, 3] if n == 4 else range(1, n):
        for j in range(swaps):
            peer = lax.rem(me + d, n)
            copy = pltpu.make_async_remote_copy(
                xs[j].at[peer // shares[j]], ys[j].at[me], send.at[j, d], recv.at[j, d],
                device_id={"samp": peer}, device_id_type=mesh)
            copy.start()
            copies.append(copy)
    for j in range(count):
        if j < swaps:
            copy = pltpu.make_async_copy(xs[j].at[me // shares[j]], ys[j].at[me], own.at[j])
        else:
            copy = pltpu.make_async_copy(xs[j], ys[j].at[1], own.at[j])
        copy.start()
        locals_.append(copy)
    for copy in locals_ + copies:
        copy.wait()
    for up, down in zip(ups, downs):
        pl.when(has_high)(up.wait_send)
        pl.when(has_low)(down.wait_send)
        pl.when(has_low)(up.wait_recv)
        pl.when(has_high)(down.wait_recv)


def exchange(number, swaps, halos):
    n, runs = lax.axis_size("samp"), lax.axis_size("box")
    arrays = [x for x, _ in swaps] + list(halos)
    shapes = [jax.ShapeDtypeStruct((n,) + x.shape[1:], x.dtype) for x, _ in swaps]
    shapes += [jax.ShapeDtypeStruct((3,) + x.shape, x.dtype) for x in halos]
    dma = pltpu.SemaphoreType.DMA
    return pl.pallas_call(
        functools.partial(
            exchange_kernel, n, runs, len(swaps), len(halos), tuple(s for _, s in swaps)),
        in_specs=[pl.BlockSpec(memory_space=pl.ANY)] * len(arrays),
        out_specs=[pl.BlockSpec(memory_space=pl.ANY)] * len(arrays),
        out_shape=shapes,
        scratch_shapes=[
            dma((max(len(swaps), 1), n)),
            dma((max(len(swaps), 1), n)),
            dma((len(arrays),)),
            dma((max(len(halos), 1), 2)),
            dma((max(len(halos), 1), 2)),
        ],
        compiler_params=pltpu.CompilerParams(
            collective_id=number, has_side_effects=True, vmem_limit_bytes=GRANT),
    )(*arrays)


def ranks(key):
    count = key.shape[0]
    ids = jnp.arange(count, dtype=jnp.int32)
    before = (key[None, :] < key[:, None]) | (
        (key[None, :] == key[:, None]) & (ids[None, :] < ids[:, None]))
    rank = jnp.sum(before.astype(jnp.int32), axis=1)
    order = jnp.sum(jnp.where(rank[None, :] == ids[:, None], ids[None, :], 0), axis=1)
    return rank, order


def pick(values, index):
    hot = index[:, None] == jnp.arange(values.shape[0], dtype=jnp.int32)[None, :]
    return jnp.sum(jnp.where(hot, values[None, :], 0), axis=1)


def body(
    radiation, theta_mid, phi_mid, theta_top, phi_top, shift_mid, shift_top,
    octant_low, octant_mid, parent_low, parent_mid, trans_low, trans_mid, trans_top,
    far_low, far_mid, far_top, offset_low, offset_mid, offset_top,
):
    n = lax.axis_size("samp")
    me, box = lax.axis_index("samp"), lax.axis_index("box")
    lows, mids = octant_low.shape[0], octant_mid.shape[0]
    tops = mids // 4
    low_each, mid_each = lows // n, mids // n
    _, _, rows_low, p_low = radiation.shape
    rank_mid, order_mid = ranks(parent_mid)
    rank_low, order_low = ranks(pick(rank_mid, parent_low - box * mids))
    oct_low = lax.dynamic_slice_in_dim(pick(octant_low, order_low), me * low_each, low_each)
    oct_mid = lax.dynamic_slice_in_dim(pick(octant_mid, order_mid), me * mid_each, mid_each)

    grouped = jnp.take(radiation, order_low, axis=1)
    grouped = jnp.moveaxis(grouped.reshape(2, n, low_each, rows_low, p_low), 1, 0)
    low_parts, near_low = exchange(0, [(grouped, 1)], [radiation])
    mid_parts = go_up(low_parts, theta_mid, phi_mid, shift_mid, oct_low, mid_each)
    top_here, mid_here = middle_stage(
        2, mid_parts, oct_mid, theta_top, phi_top, shift_top, rank_mid, trans_mid, trans_top,
        entries(far_mid, mids)[order_mid], offset_mid[order_mid],
        entries(far_top, tops), offset_top)
    mid_in = go_down(top_here, theta_top, phi_top, shift_top, oct_mid, mid_here)
    low_in = go_down(mid_in, theta_mid, phi_mid, shift_mid, oct_low, None)
    return last_stage(
        3, low_in, near_low, trans_low, entries(far_low, lows), offset_low, rank_low)


def solution(mesh):
    in_specs = (
        P(None, "box", "samp", None),
        P(), P(), P(), P(), P(), P(),
        P("box"), P("box"), P("box"), P("box"),
        P(None, None, "samp", None),
        P(None, None, "samp", None),
        P(None, None, "samp", None),
        P("box", None), P("box", None), P("box", None),
        P("box", None), P("box", None), P("box", None),
    )
    out_specs = P(None, "box", "samp", None)
    return jax.shard_map(body, mesh=mesh, in_specs=in_specs, out_specs=out_specs, check_vma=False)
```
